256 devices in a mesh: bx: 16 (over y, x_hi, core), by: 16 (over z, x_lo).
Axes of the slice: x: 4 (x_hi: 2, x_lo: 2; x = x_hi * 2 + x_lo), y: 4, z: 8, core: 2. Of those that a mesh axis runs over, the one named last changes fastest.
Arguments:
- points: bfloat16 [16, 16384, 512], P('by', 'bx'), may hold values from -6 to 6
- voxel_index: int32 [16, 16384], P('by', 'bx'), may hold values from 0 to 2047, as said below
- counts: int32 [16, 16], P('by', 'bx'), may hold values from 576 to 1024, as said below
- cpe_depth: bfloat16 [27, 512], replicated, may hold values from -2.5 to 2.5
- cpe_weight: bfloat16 [512, 512], replicated, may hold values from -0.25 to 0.25
- cpe_gain: bfloat16 [512], replicated, may hold values from 0.099609375 to 1.8984375
- norm1_gain: bfloat16 [512], replicated, may hold values from 0.099609375 to 1.8984375
- qkv_weight: bfloat16 [512, 1536], replicated
- proj_weight: bfloat16 [512, 512], replicated, may hold values from -0.25 to 0.25
- norm2_gain: bfloat16 [512], replicated, may hold values from 0.099609375 to 1.8984375
- mlp_in: bfloat16 [512, 2048], replicated, may hold values from -0.25 to 0.25
- mlp_out: bfloat16 [2048, 512], replicated, may hold values from -0.125 to 0.125
Outputs:
- block_out: bfloat16 [16, 16384, 512], P('by', 'bx')
The draws below stay inside these ranges and needn't reach their ends.
Inputs may be any that keep to these rules, and one draw needn't show every extreme that they name: `voxel_index`: within one brick the 1024 slots name different voxels. `counts`: some brick of every chain is full.
All inputs are finite; a program needn't handle non-finite values.
Results may differ from the reference program's by a relative error of at most 0.012.
The reference program's roundings to bfloat16 on the way count: a program that leaves them out, or rounds other values in their place, can miss the bound.
Values may be sent and summed in bfloat16 or wider, within the bound.
A program may use at most 128 MiB of HBM per device.

```python
import jax
import jax.numpy as jnp
from jax import lax

C = 512
HEADS = 32
HEAD_DIM = 16
MLP_WIDTH = 2048
PATCH = 1024
HALF = 512
P_DEV = 1024
VX = 8
VY = 16
VZ = 16
VOX = 2048
CHAINS = 16
CHAIN_DEV = 16
CHAIN_PTS = 16384


def draw_voxel_index(key, part):
    keys_all = jax.random.split(key, CHAINS * CHAIN_DEV)
    chosen = jax.vmap(lambda sub_key: jax.random.permutation(sub_key, VOX)[:P_DEV])(keys_all)
    return chosen.reshape(CHAINS, CHAIN_DEV * P_DEV).astype(jnp.int32)


def draw_counts(key, part):
    first_key, second_key = jax.random.split(key)
    lowest = P_DEV - HALF + HALF // 8
    values = jax.random.randint(first_key, (CHAINS, CHAIN_DEV), lowest, P_DEV + 1)
    picked = jax.random.randint(second_key, (CHAINS,), 0, CHAIN_DEV)
    columns = jnp.arange(CHAIN_DEV, dtype=jnp.int32)
    return jnp.where(columns[None, :] == picked[:, None], P_DEV, values).astype(jnp.int32)


def draw_qkv_weight(key, part):
    key_a, key_b, key_c = jax.random.split(key, 3)
    scale = C ** (-0.5)
    base = jax.random.normal(key_a, (C, C), jnp.float32) * scale
    other = jax.random.normal(key_b, (C, C), jnp.float32) * scale
    value_part = jax.random.normal(key_c, (C, C), jnp.float32) * scale
    query_part = base
    key_part = other
    return jnp.concatenate([query_part, key_part, value_part], axis=1).astype(jnp.bfloat16)


def levels(rng, extent, cuts, least, largest):
    factor_of, own = 1.0, jax.random.fold_in(rng, 6)
    for position, shards_of in cuts:
        heights = jnp.exp(jax.random.uniform(jax.random.fold_in(own, position), (shards_of,), jnp.float32, least / len(cuts), largest / len(cuts)))
        factor_of = factor_of * jnp.repeat(heights, extent[position] // shards_of).reshape([-1 if axis == position else 1 for axis in range(len(extent))])
    return factor_of


def bell_draw(own_key, shape, scale, bound, shards=(), held_as=jnp.bfloat16):
    loudness = levels(own_key, shape, shards, -0.22, 0.18) if shards else 1.0
    values = jax.random.normal(own_key, shape, jnp.float32) * scale * loudness
    return jnp.minimum(jnp.maximum(values, -bound), bound).astype(held_as)


def setup_inputs(seed: int = 0) -> dict:
    key_of = jax.random.split(jax.random.key(seed), 13)
    return {
        "points": bell_draw(key_of[0], (CHAINS, CHAIN_PTS, C), 1.0, 6.0, ((0, 16), (1, 16))),
        "voxel_index": draw_voxel_index(jax.random.fold_in(key_of[12], 71), 0),
        "counts": draw_counts(jax.random.fold_in(key_of[12], 71), 0),
        "cpe_depth": bell_draw(key_of[3], (27, C), 0.3, 2.5),
        "cpe_weight": bell_draw(key_of[4], (C, C), C ** -0.5, 0.25),
        "cpe_gain": jnp.clip(1.0 + 0.18 * jax.random.normal(key_of[5], (C,), jnp.float32), 0.099609375, 1.8984375).astype(jnp.bfloat16),
        "norm1_gain": jnp.clip(1.0 + 0.18 * jax.random.normal(key_of[6], (C,), jnp.float32), 0.099609375, 1.8984375).astype(jnp.bfloat16),
        "qkv_weight": draw_qkv_weight(jax.random.fold_in(key_of[12], 71), 0),
        "proj_weight": bell_draw(key_of[8], (C, C), C ** -0.5, 0.25),
        "norm2_gain": jnp.clip(1.0 + 0.18 * jax.random.normal(key_of[9], (C,), jnp.float32), 0.099609375, 1.8984375).astype(jnp.bfloat16),
        "mlp_in": bell_draw(key_of[10], (C, MLP_WIDTH), C ** -0.5, 0.25),
        "mlp_out": bell_draw(key_of[11], (MLP_WIDTH, C), MLP_WIDTH ** -0.5, 0.125),
    }


def layer_norm(values):
    center = values - lax.optimization_barrier(jnp.mean(values, axis=-1, keepdims=True))
    spread = lax.optimization_barrier(jnp.mean(center * center, axis=-1, keepdims=True))
    return center * lax.rsqrt(spread + 1e-05)

def reference(points, voxel_index, counts, cpe_depth, cpe_weight, cpe_gain, norm1_gain, qkv_weight, proj_weight, norm2_gain, mlp_in, mlp_out):
    feats = points.reshape(CHAINS, CHAIN_DEV, P_DEV, C)
    voxels = voxel_index.reshape(CHAINS, CHAIN_DEV, P_DEV)
    row_ids = jnp.arange(P_DEV, dtype=jnp.int32)
    valid = row_ids[None, None, :] < counts[:, :, None]
    target = jnp.where(valid, voxels, VOX).astype(jnp.int32)

    def place(rows, where_to):
        return jnp.zeros((VOX, C), jnp.bfloat16).at[where_to].set(rows, mode='drop')
    grid = jax.vmap(jax.vmap(place))(feats, target)
    grid = grid.reshape(CHAINS, CHAIN_DEV, VX, VY, VZ, C).transpose(1, 2, 0, 3, 4, 5)
    grid = grid.reshape(CHAIN_DEV * VX, CHAINS * VY, VZ, C)
    padded = jnp.pad(grid, ((1, 1), (1, 1), (1, 1), (0, 0)))
    depth = cpe_depth.astype(jnp.float32)
    width_y = CHAINS * VY

    def plane(index):
        slab = lax.dynamic_slice_in_dim(padded, index, 3, 0).astype(jnp.float32)
        total = jnp.zeros((width_y, VZ, C), jnp.float32)
        for off_x in range(3):
            for off_y in range(3):
                for off_z in range(3):
                    number = 9 * off_x + 3 * off_y + off_z
                    total = total + slab[off_x, off_y:off_y + width_y, off_z:off_z + VZ] * depth[number]
        return total.astype(jnp.bfloat16)
    conv = lax.map(plane, jnp.arange(CHAIN_DEV * VX, dtype=jnp.int32))
    conv = conv.reshape(CHAIN_DEV, VX, CHAINS, VY, VZ, C).transpose(2, 0, 1, 3, 4, 5)
    conv = conv.reshape(CHAINS, CHAIN_DEV, VOX, C)
    pos = jax.vmap(jax.vmap(lambda table, index: table[index]))(conv, voxels)
    n_patch = CHAIN_PTS // PATCH

    def one_patch(items):
        queries, key_rows, value_rows, key_ok = items
        scores = jnp.einsum('qhd,khd->hqk', queries.astype(jnp.float32), key_rows.astype(jnp.float32)) * 0.25
        scores = jnp.where(key_ok[None, None, :], scores, -1e+30)
        top = lax.optimization_barrier(jnp.max(scores, axis=-1, keepdims=True))
        expo = jnp.exp(scores - top)
        probs = (expo / lax.optimization_barrier(jnp.sum(expo, axis=-1, keepdims=True))).astype(jnp.bfloat16)
        result = jnp.einsum('hqk,khd->qhd', probs.astype(jnp.float32), value_rows.astype(jnp.float32))
        return result.astype(jnp.bfloat16).reshape(PATCH, C)

    def chain(items):
        chain_x, chain_pos, chain_ok = items
        branch = layer_norm(jnp.dot(chain_pos, cpe_weight, preferred_element_type=jnp.float32)) * cpe_gain.astype(jnp.float32)
        first = (chain_x.astype(jnp.float32) + branch).astype(jnp.bfloat16)
        normed = (layer_norm(first.astype(jnp.float32)) * norm1_gain.astype(jnp.float32)).astype(jnp.bfloat16)
        projected = jnp.dot(normed, qkv_weight, preferred_element_type=jnp.float32).astype(jnp.bfloat16)
        rolled = jnp.concatenate([projected[HALF:], projected[:HALF]], axis=0)
        rolled_ok = jnp.concatenate([chain_ok[HALF:], chain_ok[:HALF]], axis=0)
        queries = rolled[:, :C].reshape(n_patch, PATCH, HEADS, HEAD_DIM)
        key_rows = rolled[:, C:2 * C].reshape(n_patch, PATCH, HEADS, HEAD_DIM)
        value_rows = rolled[:, 2 * C:].reshape(n_patch, PATCH, HEADS, HEAD_DIM)
        attended = lax.map(one_patch, (queries, key_rows, value_rows, rolled_ok.reshape(n_patch, PATCH)))
        attended = attended.reshape(CHAIN_PTS, C)
        attended = jnp.concatenate([attended[CHAIN_PTS - HALF:], attended[:CHAIN_PTS - HALF]], axis=0)
        second = (first.astype(jnp.float32) + jnp.dot(attended, proj_weight, preferred_element_type=jnp.float32)).astype(jnp.bfloat16)
        normed_two = (layer_norm(second.astype(jnp.float32)) * norm2_gain.astype(jnp.float32)).astype(jnp.bfloat16)
        hidden = jax.nn.gelu(jnp.dot(normed_two, mlp_in, preferred_element_type=jnp.float32), approximate=False).astype(jnp.bfloat16)
        final = (second.astype(jnp.float32) + jnp.dot(hidden, mlp_out, preferred_element_type=jnp.float32)).astype(jnp.bfloat16)
        return jnp.where(chain_ok[:, None], final, jnp.zeros_like(final))
    return lax.map(chain, (points, pos.reshape(CHAINS, CHAIN_PTS, C), valid.reshape(CHAINS, CHAIN_PTS)))
```

```python
import jax
import jax.numpy as jnp
from jax import lax
from jax.experimental import pallas as pl
from jax.experimental.pallas import tpu as pltpu
from jax.sharding import PartitionSpec as P

MESH = pl.DeviceIdType.MESH
BF = jnp.bfloat16
F32 = jnp.float32
C = 512
HEADS = 32
ROWS = 1024
HALF = 512
VX = 8
VY = 16
VZ = 16
VOX = 2048
PLANE = VY * VZ
NEG = -1e30
CQ = 256
UNROLL = 4


def dot(a, b):
    return jnp.dot(a, b, preferred_element_type=F32)


def dot_nt(a, b):
    return lax.dot_general(a, b, (((1,), (1,)), ((), ())), preferred_element_type=F32)


def dot_tn(a, b):
    return lax.dot_general(a, b, (((0,), (0,)), ((), ())), preferred_element_type=F32)


def layer_norm(values):
    center = values - jnp.mean(values, axis=-1, keepdims=True)
    spread = jnp.mean(center * center, axis=-1, keepdims=True)
    return center * lax.rsqrt(spread + 1e-05)


def front_kernel(
    points,
    voxels,
    counts,
    depth,
    cpe_w_hbm,
    cpe_gain,
    gain1,
    qkv_hbm,
    proj_hbm,
    second,
    feats,
    cpe_w,
    qkv_w,
    proj_w,
    wt,
    grid,
    taps,
    conv,
    first,
    normed,
    far,
    qt,
    keys,
    vt,
    far_keys,
    far_vt,
    bias,
    ones_row,
    scores,
    tops,
    part_o,
    part_ml,
    att,
    count_out,
    count_in,
    load_sem,
    send_sem,
    recv_sem,
):
    bx, by = lax.axis_index("bx"), lax.axis_index("by")
    n_bx, n_by = lax.axis_size("bx"), lax.axis_size("by")
    low_x, high_x = lax.rem(bx + n_bx - 1, n_bx), lax.rem(bx + 1, n_bx)
    low_y, high_y = lax.rem(by + n_by - 1, n_by), lax.rem(by + 1, n_by)

    def at(x, y):
        return {"bx": x, "by": y}

    around = [
        (low_x, by),
        (high_x, by),
        (bx, low_y),
        (bx, high_y),
        (low_x, low_y),
        (low_x, high_y),
        (high_x, low_y),
        (high_x, high_y),
    ]
    barrier = pltpu.get_barrier_semaphore()
    for x, y in around:
        pl.semaphore_signal(barrier, inc=1, device_id=at(x, y), device_id_type=MESH)

    loads = [
        pltpu.make_async_copy(source, held, load_sem.at[i])
        for i, (source, held) in enumerate(
            (
                (points.at[0], feats),
                (cpe_w_hbm, cpe_w),
                (qkv_hbm, qkv_w),
                (proj_hbm, proj_w),
            )
        )
    ]
    for load in loads:
        load.start()

    def remote(i, source, target, where):
        return pltpu.make_async_remote_copy(
            src_ref=source,
            dst_ref=target,
            send_sem=send_sem.at[i],
            recv_sem=recv_sem.at[i],
            device_id=at(*where),
            device_id_type=MESH,
        )

    inner_y = pl.ds(1, VY)
    inner_x = pl.ds(1, VX)
    halo_x = [
        remote(0, grid.at[1, inner_y], grid.at[VX + 1, inner_y], (low_x, by)),
        remote(1, grid.at[VX, inner_y], grid.at[0, inner_y], (high_x, by)),
        remote(2, grid.at[1, 1], grid.at[VX + 1, VY + 1], (low_x, low_y)),
        remote(3, grid.at[1, VY], grid.at[VX + 1, 0], (low_x, high_y)),
        remote(4, grid.at[VX, 1], grid.at[0, VY + 1], (high_x, low_y)),
        remote(5, grid.at[VX, VY], grid.at[0, 0], (high_x, high_y)),
        remote(6, count_out, count_in, (high_x, by)),
    ]
    halo_y = [
        remote(7, grid.at[inner_x, 1], grid.at[inner_x, VY + 1], (bx, low_y)),
        remote(8, grid.at[inner_x, VY], grid.at[inner_x, 0], (bx, high_y)),
    ]
    low_half, high_half = pl.ds(0, HALF), pl.ds(HALF, HALF)
    to_low = remote(9, normed.at[low_half], far.at[high_half], (low_x, by))
    to_high = remote(10, normed.at[high_half], far.at[low_half], (high_x, by))

    count = counts[...].astype(F32)
    count_out[...] = jnp.broadcast_to(count, (8, 128))
    slot = lax.broadcasted_iota(jnp.int32, (1, ROWS), 1)
    where_to = jnp.where(slot.astype(F32) < count, voxels[...], VOX)

    loads[0].wait()

    def scatter(plane):
        row = lax.broadcasted_iota(jnp.int32, (PLANE, ROWS), 0) + plane * PLANE
        hot = jnp.where(row == where_to, 1.0, 0.0).astype(BF)
        grid[plane + 1, 1 : VY + 1] = dot(hot, feats[...]).astype(BF).reshape(VY, VZ, C)

    scatter(0)
    scatter(VX - 1)
    pl.semaphore_wait(barrier, 8)
    for copy in halo_x:
        copy.start()

    def scatter_step(plane, carry):
        scatter(plane)
        return carry

    lax.fori_loop(1, VX - 1, scatter_step, 0)
    for copy in halo_y:
        copy.start()

    taps[...] = depth[...].astype(F32)

    def conv_rows(x, lanes, y_first, y_count):
        weight = [taps[pl.ds(i, 1), lanes] for i in range(27)]
        z = lax.broadcasted_iota(jnp.int32, (VZ, 128), 0)
        parts = [[None] * 3 for _ in range(y_count)]
        for off_x in range(3):
            for row in range(y_count + 2):
                block = grid[x + off_x, y_first + row, :, lanes].astype(F32)
                for i in range(y_count):
                    off_y = row - i
                    if 0 <= off_y <= 2:
                        for off_z in range(3):
                            term = block * weight[9 * off_x + 3 * off_y + off_z]
                            held = parts[i][off_z]
                            parts[i][off_z] = term if held is None else held + term
        for i in range(y_count):
            before, same, after = parts[i]
            before = jnp.where(z == 0, 0.0, pltpu.roll(before, 1, 0))
            after = jnp.where(z == VZ - 1, 0.0, pltpu.roll(after, VZ - 1, 0))
            start = pl.multiple_of(x * PLANE + (y_first + i) * VZ, VZ)
            conv[pl.ds(start, VZ), lanes] = (before + same + after).astype(BF)

    def inner_step(i, carry):
        lanes = pl.ds(pl.multiple_of(lax.rem(i, 4) * 128, 128), 128)
        for y in range(1, VY - 1, 2):
            conv_rows(lax.div(i, 4) + 1, lanes, y, 2)
        return carry

    lax.fori_loop(0, 4 * (VX - 2), inner_step, 0)

    loads[1].wait()
    loads[2].wait()
    loads[3].wait()
    wt[0:C] = qkv_w[:, 0:C].T
    wt[C : 2 * C] = qkv_w[:, 2 * C : 3 * C].T

    for copy in halo_x + halo_y:
        copy.wait()
    zero_x = jnp.zeros((VY + 2, VZ, C), BF)
    zero_y = jnp.zeros((VX + 2, VZ, C), BF)

    @pl.when(bx == 0)
    def _():
        grid[0] = zero_x

    @pl.when(bx == n_bx - 1)
    def _():
        grid[VX + 1] = zero_x

    @pl.when(by == 0)
    def _():
        grid[:, 0] = zero_y

    @pl.when(by == n_by - 1)
    def _():
        grid[:, VY + 1] = zero_y

    def outer_step(i, carry):
        lanes = pl.ds(pl.multiple_of(lax.rem(i, 4) * 128, 128), 128)
        for y in range(0, VY, 2):
            conv_rows(lax.div(i, 4) * (VX - 1), lanes, y, 2)
        return carry

    lax.fori_loop(0, 8, outer_step, 0)

    def side_step(i, carry):
        lanes = pl.ds(pl.multiple_of(lax.rem(i, 4) * 128, 128), 128)
        for y in (0, VY - 1):
            conv_rows(lax.div(i, 4) + 1, lanes, y, 1)
        return carry

    lax.fori_loop(0, 4 * (VX - 2), side_step, 0)

    def gather(half):
        total = None
        for part in range(4):
            lane = lax.broadcasted_iota(jnp.int32, (HALF, HALF), 1) + part * HALF
            column = jnp.concatenate(
                [
                    jnp.broadcast_to(
                        voxels[:, half * HALF + i * 128 : half * HALF + (i + 1) * 128].astype(F32),
                        (128, 128),
                    ).T
                    for i in range(4)
                ],
                axis=0,
            ).astype(jnp.int32)
            hot = jnp.where(jnp.concatenate([column] * 4, axis=1) == lane, 1.0, 0.0).astype(BF)
            term = dot(hot, conv[part * HALF : (part + 1) * HALF])
            total = term if total is None else total + term
        rows = slice(half * HALF, (half + 1) * HALF)
        branch = layer_norm(dot(total.astype(BF), cpe_w[...])) * cpe_gain[...].astype(F32)
        here = (feats[rows].astype(F32) + branch).astype(BF)
        first[rows] = here
        normed[rows] = (layer_norm(here.astype(F32)) * gain1[...].astype(F32)).astype(BF)

    gather(0)
    to_low.start()
    gather(1)
    to_high.start()

    qt[...] = (dot_nt(wt[0:C], normed[...]).astype(BF).astype(F32) * 0.25).astype(BF)
    keys[...] = dot(normed[...], qkv_w[:, C : 2 * C]).astype(BF)
    vt[...] = dot_nt(wt[C : 2 * C], normed[...]).astype(BF)

    row_id = (lax.broadcasted_iota(jnp.int32, (HALF, 128), 0) + HALF).astype(F32)
    lane_id = lax.broadcasted_iota(jnp.int32, (HALF, 128), 1)
    bias[0] = jnp.where((lane_id == 0) & (row_id >= count), NEG, 0.0).astype(BF)
    bias[1] = jnp.where((lane_id == 0) & (row_id >= count_in[0:1, :]), NEG, 0.0).astype(BF)
    ones_row[...] = jnp.where(
        lax.broadcasted_iota(jnp.int32, (128, CQ), 0) == 0, 1.0, 0.0
    ).astype(BF)

    lane_head = lax.broadcasted_iota(jnp.int32, (1, 128), 1) // 16
    ones16 = jnp.ones((16, HALF), BF)

    def attention(k_ref, v_ref, biased, which, finish):
        def step(h, before, now):
            other = 1 - now
            lanes = pl.ds(pl.multiple_of(lax.div(h, 8) * 128, 128), 128)
            mine = lane_head == lax.rem(h, 8)
            if before is not None:
                head_rows = pl.ds(pl.multiple_of(before * 16, 16), 16)
            for b in range(2):
                rows = slice(b * HALF, (b + 1) * HALF)
                k_h = k_ref[rows, lanes]
                k_h = jnp.where(mine, k_h, jnp.zeros_like(k_h))
                if b == biased:
                    k_h = jnp.concatenate([k_h, bias[which]], axis=1)
                if before is not None:
                    w = jnp.concatenate([v_ref[head_rows, rows], ones16], axis=0)
                for part in range(HALF // CQ):
                    cols = slice(b * HALF + part * CQ, b * HALF + (part + 1) * CQ)
                    q_g = qt[lanes, cols]
                    if b == biased:
                        q_g = jnp.concatenate([q_g, ones_row[...]], axis=0)
                    s = dot(k_h, q_g)
                    scores[now, :, cols] = s
                    tops[now, 0:1, cols] = jnp.max(s, axis=0, keepdims=True)
                    if before is not None:
                        top = tops[other, 0:1, cols]
                        p = jnp.exp(scores[other, :, cols] - top).astype(BF)
                        finish(before, head_rows, cols, top, dot(w, p))

        step(0, None, 0)

        def body(i, carry):
            for u in range(UNROLL):
                before = i * UNROLL + u
                step(jnp.minimum(before + 1, HEADS - 1), before, (u + 1) % 2)
            return carry

        lax.fori_loop(0, HEADS // UNROLL, body, 0)

    def keep(h, head_rows, cols, top, acc):
        part_o[head_rows, cols] = acc[0:16]
        part_ml[h, 0:1, cols] = top
        part_ml[h, 1:2, cols] = acc[16:17]

    attention(keys, vt, 1, 0, keep)

    to_low.wait()
    to_high.wait()
    far_keys[...] = dot(far[...], qkv_w[:, C : 2 * C]).astype(BF)
    far_vt[...] = dot_nt(wt[C : 2 * C], far[...]).astype(BF)

    def merge(h, head_rows, cols, top, acc):
        near_top = part_ml[h, 0:1, cols]
        both = jnp.maximum(near_top, top)
        near, here = jnp.exp(near_top - both), jnp.exp(top - both)
        total = part_ml[h, 1:2, cols] * near + acc[16:17] * here
        att[head_rows, cols] = ((part_o[head_rows, cols] * near + acc[0:16] * here) / total).astype(BF)

    attention(far_keys, far_vt, 0, 1, merge)

    second[...] = (first[...].astype(F32) + dot_tn(att[...], proj_w[...])).astype(BF)


def erf(x):
    size = jnp.abs(x)
    t = 1.0 / (1.0 + 0.3275911 * size)
    poly = t * (
        0.254829592
        + t * (-0.284496736 + t * (1.421413741 + t * (-1.453152027 + t * 1.061405429)))
    )
    value = 1.0 - poly * jnp.exp(-size * size)
    return jnp.where(x < 0, -value, value)


def gelu(x):
    return 0.5 * x * (1.0 + erf(x * 0.7071067811865476))


def back_kernel(second, counts, gain2, mlp_in, mlp_out, out):
    tile = 256
    count = counts[...].astype(F32)

    def step(i, carry):
        rows = pl.ds(pl.multiple_of(i * tile, tile), tile)
        here = second[rows, :].astype(F32)
        normed = (layer_norm(here) * gain2[...].astype(F32)).astype(BF)
        total = here
        for part in range(4):
            cols = slice(part * 512, (part + 1) * 512)
            hidden = gelu(dot(normed, mlp_in[:, cols])).astype(BF)
            total = total + dot(hidden, mlp_out[cols, :])
        row_id = (lax.broadcasted_iota(jnp.int32, (tile, C), 0) + i * tile).astype(F32)
        out[0, rows, :] = jnp.where(row_id < count, total, 0.0).astype(BF)
        return carry

    lax.fori_loop(0, ROWS // tile, step, 0)


def per_device(
    points,
    voxel_index,
    counts,
    cpe_depth,
    cpe_weight,
    cpe_gain,
    norm1_gain,
    qkv_weight,
    proj_weight,
    norm2_gain,
    mlp_in,
    mlp_out,
):
    vmem = pl.BlockSpec(memory_space=pltpu.VMEM)
    hbm = pl.BlockSpec(memory_space=pl.ANY)
    second = pl.pallas_call(
        front_kernel,
        out_shape=jax.ShapeDtypeStruct((ROWS, C), BF),
        in_specs=[hbm, vmem, vmem, vmem, hbm, vmem, vmem, hbm, hbm],
        out_specs=vmem,
        scratch_shapes=[
            pltpu.VMEM((ROWS, C), BF),
            pltpu.VMEM((C, C), BF),
            pltpu.VMEM((C, 3 * C), BF),
            pltpu.VMEM((C, C), BF),
            pltpu.VMEM((2 * C, C), BF),
            pltpu.VMEM((VX + 2, VY + 2, VZ, C), BF),
            pltpu.VMEM((27, C), F32),
            pltpu.VMEM((VOX, C), BF),
            pltpu.VMEM((ROWS, C), BF),
            pltpu.VMEM((ROWS, C), BF),
            pltpu.VMEM((ROWS, C), BF),
            pltpu.VMEM((C, ROWS), BF),
            pltpu.VMEM((ROWS, C), BF),
            pltpu.VMEM((C, ROWS), BF),
            pltpu.VMEM((ROWS, C), BF),
            pltpu.VMEM((C, ROWS), BF),
            pltpu.VMEM((2, HALF, 128), BF),
            pltpu.VMEM((128, CQ), BF),
            pltpu.VMEM((2, HALF, ROWS), F32),
            pltpu.VMEM((2, 8, ROWS), F32),
            pltpu.VMEM((C, ROWS), F32),
            pltpu.VMEM((HEADS, 8, ROWS), F32),
            pltpu.VMEM((C, ROWS), BF),
            pltpu.VMEM((8, 128), F32),
            pltpu.VMEM((8, 128), F32),
            pltpu.SemaphoreType.DMA((4,)),
            pltpu.SemaphoreType.DMA((11,)),
            pltpu.SemaphoreType.DMA((11,)),
        ],
        compiler_params=pltpu.CompilerParams(
            collective_id=0, has_side_effects=True, vmem_limit_bytes=48 * 2**20
        ),
        name="front",
    )(
        points,
        voxel_index,
        counts,
        cpe_depth,
        cpe_weight,
        cpe_gain.reshape(1, C),
        norm1_gain.reshape(1, C),
        qkv_weight,
        proj_weight,
    )
    return pl.pallas_call(
        back_kernel,
        out_shape=jax.ShapeDtypeStruct((1, ROWS, C), BF),
        in_specs=[vmem] * 5,
        out_specs=vmem,
        compiler_params=pltpu.CompilerParams(vmem_limit_bytes=48 * 2**20),
        name="back",
    )(second, counts, norm2_gain.reshape(1, C), mlp_in, mlp_out)


def solution(mesh):
    in_specs = (P("by", "bx", None), P("by", "bx"), P("by", "bx")) + (P(),) * 9
    return jax.shard_map(
        per_device,
        mesh=mesh,
        in_specs=in_specs,
        out_specs=P("by", "bx", None),
        check_vma=False,
    )
```

```python
import jax
import jax.numpy as jnp
from jax import lax
from jax.experimental import pallas as pl
from jax.experimental.pallas import tpu as pltpu
from jax.sharding import PartitionSpec as P

MESH = pl.DeviceIdType.MESH
BF = jnp.bfloat16
F32 = jnp.float32
C = 512
HEADS = 32
ROWS = 1024
HALF = 512
VX = 8
VY = 16
VZ = 16
VOX = 2048
PLANE = VY * VZ
NEG = -1e30
CQ = 256
UNROLL = 4


def dot(a, b):
    return jnp.dot(a, b, preferred_element_type=F32)


def dot_nt(a, b):
    return lax.dot_general(a, b, (((1,), (1,)), ((), ())), preferred_element_type=F32)


def dot_tn(a, b):
    return lax.dot_general(a, b, (((0,), (0,)), ((), ())), preferred_element_type=F32)


def layer_norm(values):
    center = values - jnp.mean(values, axis=-1, keepdims=True)
    spread = jnp.mean(center * center, axis=-1, keepdims=True)
    return center * lax.rsqrt(spread + 1e-05)


def front_kernel(
    points_hbm,
    voxels_hbm,
    counts_hbm,
    depth_hbm,
    cpe_w_hbm,
    cpe_gain_hbm,
    gain1_hbm,
    qkv_hbm,
    proj_hbm,
    gain2_hbm,
    second,
    aside,
    feats,
    voxels,
    counts,
    depth,
    cpe_gain,
    gain1,
    gain2,
    cpe_w,
    qkv_w,
    proj_w,
    wt,
    grid,
    taps,
    conv,
    first,
    normed,
    far,
    qt,
    keys,
    vt,
    far_keys,
    far_vt,
    bias,
    ones_row,
    scores,
    tops,
    part_o,
    part_ml,
    att,
    count_out,
    count_in,
    load_sem,
    send_sem,
    recv_sem,
):
    bx, by = lax.axis_index("bx"), lax.axis_index("by")
    n_bx, n_by = lax.axis_size("bx"), lax.axis_size("by")
    low_x, high_x = lax.rem(bx + n_bx - 1, n_bx), lax.rem(bx + 1, n_bx)
    low_y, high_y = lax.rem(by + n_by - 1, n_by), lax.rem(by + 1, n_by)

    def at(x, y):
        return {"bx": x, "by": y}

    around = [
        (low_x, by),
        (high_x, by),
        (bx, low_y),
        (bx, high_y),
        (low_x, low_y),
        (low_x, high_y),
        (high_x, low_y),
        (high_x, high_y),
    ]
    barrier = pltpu.get_barrier_semaphore()
    for x, y in around:
        pl.semaphore_signal(barrier, inc=1, device_id=at(x, y), device_id_type=MESH)

    loads = [
        pltpu.make_async_copy(source, held, load_sem.at[i])
        for i, (source, held) in enumerate(
            (
                (voxels_hbm, voxels),
                (counts_hbm, counts),
                (points_hbm.at[0], feats),
                (depth_hbm, depth),
                (cpe_gain_hbm, cpe_gain),
                (gain1_hbm, gain1),
                (gain2_hbm, gain2),
                (cpe_w_hbm, cpe_w),
                (qkv_hbm, qkv_w),
                (proj_hbm, proj_w),
            )
        )
    ]
    for load in loads:
        load.start()

    def remote(i, source, target, where):
        return pltpu.make_async_remote_copy(
            src_ref=source,
            dst_ref=target,
            send_sem=send_sem.at[i],
            recv_sem=recv_sem.at[i],
            device_id=at(*where),
            device_id_type=MESH,
        )

    inner_y = pl.ds(1, VY)
    inner_x = pl.ds(1, VX)
    halo_x = [
        remote(0, grid.at[1, inner_y], grid.at[VX + 1, inner_y], (low_x, by)),
        remote(1, grid.at[VX, inner_y], grid.at[0, inner_y], (high_x, by)),
        remote(2, grid.at[1, 1], grid.at[VX + 1, VY + 1], (low_x, low_y)),
        remote(3, grid.at[1, VY], grid.at[VX + 1, 0], (low_x, high_y)),
        remote(4, grid.at[VX, 1], grid.at[0, VY + 1], (high_x, low_y)),
        remote(5, grid.at[VX, VY], grid.at[0, 0], (high_x, high_y)),
        remote(6, count_out, count_in, (high_x, by)),
    ]
    halo_y = [
        remote(7, grid.at[inner_x, 1], grid.at[inner_x, VY + 1], (bx, low_y)),
        remote(8, grid.at[inner_x, VY], grid.at[inner_x, 0], (bx, high_y)),
    ]
    low_half, high_half = pl.ds(0, HALF), pl.ds(HALF, HALF)
    to_low = remote(9, normed.at[low_half], far.at[high_half], (low_x, by))
    to_high = remote(10, normed.at[high_half], far.at[low_half], (high_x, by))

    loads[0].wait()
    loads[1].wait()
    count = counts[...].astype(F32)
    count_out[...] = jnp.broadcast_to(count, (8, 128))
    slot = lax.broadcasted_iota(jnp.int32, (1, ROWS), 1)
    where_to = jnp.where(slot.astype(F32) < count, voxels[...], VOX)

    loads[2].wait()

    def scatter(plane):
        row = lax.broadcasted_iota(jnp.int32, (PLANE, ROWS), 0) + plane * PLANE
        hot = jnp.where(row == where_to, 1.0, 0.0).astype(BF)
        grid[plane + 1, 1 : VY + 1] = dot(hot, feats[...]).astype(BF).reshape(VY, VZ, C)

    scatter(0)
    scatter(VX - 1)
    pl.semaphore_wait(barrier, 8)
    for copy in halo_x:
        copy.start()

    def scatter_step(plane, carry):
        scatter(plane)
        return carry

    lax.fori_loop(1, VX - 1, scatter_step, 0)
    for copy in halo_y:
        copy.start()

    loads[3].wait()
    taps[...] = depth[...].astype(F32)

    def conv_rows(x, lanes, y_first, y_count):
        weight = [taps[pl.ds(i, 1), lanes] for i in range(27)]
        z = lax.broadcasted_iota(jnp.int32, (VZ, 128), 0)
        parts = [[None] * 3 for _ in range(y_count)]
        for off_x in range(3):
            for row in range(y_count + 2):
                block = grid[x + off_x, y_first + row, :, lanes].astype(F32)
                for i in range(y_count):
                    off_y = row - i
                    if 0 <= off_y <= 2:
                        for off_z in range(3):
                            term = block * weight[9 * off_x + 3 * off_y + off_z]
                            held = parts[i][off_z]
                            parts[i][off_z] = term if held is None else held + term
        for i in range(y_count):
            before, same, after = parts[i]
            before = jnp.where(z == 0, 0.0, pltpu.roll(before, 1, 0))
            after = jnp.where(z == VZ - 1, 0.0, pltpu.roll(after, VZ - 1, 0))
            start = pl.multiple_of(x * PLANE + (y_first + i) * VZ, VZ)
            conv[pl.ds(start, VZ), lanes] = (before + same + after).astype(BF)

    def inner_step(i, carry):
        lanes = pl.ds(pl.multiple_of(lax.rem(i, 4) * 128, 128), 128)
        for y in range(1, VY - 1, 2):
            conv_rows(lax.div(i, 4) + 1, lanes, y, 2)
        return carry

    lax.fori_loop(0, 4 * (VX - 2), inner_step, 0)

    for load in loads[4:]:
        load.wait()
    wt[0:C] = qkv_w[:, 0:C].T
    wt[C : 2 * C] = qkv_w[:, 2 * C : 3 * C].T

    for copy in halo_x + halo_y:
        copy.wait()
    zero_x = jnp.zeros((VY + 2, VZ, C), BF)
    zero_y = jnp.zeros((VX + 2, VZ, C), BF)

    @pl.when(bx == 0)
    def _():
        grid[0] = zero_x

    @pl.when(bx == n_bx - 1)
    def _():
        grid[VX + 1] = zero_x

    @pl.when(by == 0)
    def _():
        grid[:, 0] = zero_y

    @pl.when(by == n_by - 1)
    def _():
        grid[:, VY + 1] = zero_y

    def outer_step(i, carry):
        lanes = pl.ds(pl.multiple_of(lax.rem(i, 4) * 128, 128), 128)
        for y in range(0, VY, 2):
            conv_rows(lax.div(i, 4) * (VX - 1), lanes, y, 2)
        return carry

    lax.fori_loop(0, 8, outer_step, 0)

    def side_step(i, carry):
        lanes = pl.ds(pl.multiple_of(lax.rem(i, 4) * 128, 128), 128)
        for y in (0, VY - 1):
            conv_rows(lax.div(i, 4) + 1, lanes, y, 1)
        return carry

    lax.fori_loop(0, 4 * (VX - 2), side_step, 0)

    def gather(half):
        total = None
        for part in range(4):
            lane = lax.broadcasted_iota(jnp.int32, (HALF, HALF), 1) + part * HALF
            column = jnp.concatenate(
                [
                    jnp.broadcast_to(
                        voxels[:, half * HALF + i * 128 : half * HALF + (i + 1) * 128].astype(F32),
                        (128, 128),
                    ).T
                    for i in range(4)
                ],
                axis=0,
            ).astype(jnp.int32)
            hot = jnp.where(jnp.concatenate([column] * 4, axis=1) == lane, 1.0, 0.0).astype(BF)
            term = dot(hot, conv[part * HALF : (part + 1) * HALF])
            total = term if total is None else total + term
        rows = slice(half * HALF, (half + 1) * HALF)
        branch = layer_norm(dot(total.astype(BF), cpe_w[...])) * cpe_gain[...].reshape(1, C).astype(F32)
        here = (feats[rows].astype(F32) + branch).astype(BF)
        first[rows] = here
        normed[rows] = (layer_norm(here.astype(F32)) * gain1[...].reshape(1, C).astype(F32)).astype(BF)

    gather(0)
    to_low.start()
    gather(1)
    to_high.start()

    qt[...] = (dot_nt(wt[0:C], normed[...]).astype(BF).astype(F32) * 0.25).astype(BF)
    keys[...] = dot(normed[...], qkv_w[:, C : 2 * C]).astype(BF)
    vt[...] = dot_nt(wt[C : 2 * C], normed[...]).astype(BF)

    aside[0:1, :] = gain2[...].reshape(1, C).astype(F32)
    aside[1:2, :] = jnp.broadcast_to(count, (1, C))

    row_id = (lax.broadcasted_iota(jnp.int32, (HALF, 128), 0) + HALF).astype(F32)
    lane_id = lax.broadcasted_iota(jnp.int32, (HALF, 128), 1)
    bias[0] = jnp.where((lane_id == 0) & (row_id >= count), NEG, 0.0).astype(BF)
    bias[1] = jnp.where((lane_id == 0) & (row_id >= count_in[0:1, :]), NEG, 0.0).astype(BF)
    ones_row[...] = jnp.where(
        lax.broadcasted_iota(jnp.int32, (128, CQ), 0) == 0, 1.0, 0.0
    ).astype(BF)

    lane_head = lax.broadcasted_iota(jnp.int32, (1, 128), 1) // 16
    ones16 = jnp.ones((16, HALF), BF)

    def attention(k_ref, v_ref, biased, which, finish):
        def step(h, before, now):
            other = 1 - now
            lanes = pl.ds(pl.multiple_of(lax.div(h, 8) * 128, 128), 128)
            mine = lane_head == lax.rem(h, 8)
            if before is not None:
                head_rows = pl.ds(pl.multiple_of(before * 16, 16), 16)
            for b in range(2):
                rows = slice(b * HALF, (b + 1) * HALF)
                k_h = k_ref[rows, lanes]
                k_h = jnp.where(mine, k_h, jnp.zeros_like(k_h))
                if b == biased:
                    k_h = jnp.concatenate([k_h, bias[which]], axis=1)
                if before is not None:
                    w = jnp.concatenate([v_ref[head_rows, rows], ones16], axis=0)
                for part in range(HALF // CQ):
                    cols = slice(b * HALF + part * CQ, b * HALF + (part + 1) * CQ)
                    q_g = qt[lanes, cols]
                    if b == biased:
                        q_g = jnp.concatenate([q_g, ones_row[...]], axis=0)
                    s = dot(k_h, q_g)
                    scores[now, :, cols] = s
                    tops[now, 0:1, cols] = jnp.max(s, axis=0, keepdims=True)
                    if before is not None:
                        top = tops[other, 0:1, cols]
                        p = jnp.exp(scores[other, :, cols] - top).astype(BF)
                        finish(before, head_rows, cols, top, dot(w, p))

        step(0, None, 0)

        def body(i, carry):
            for u in range(UNROLL):
                before = i * UNROLL + u
                step(jnp.minimum(before + 1, HEADS - 1), before, (u + 1) % 2)
            return carry

        lax.fori_loop(0, HEADS // UNROLL, body, 0)

    def keep(h, head_rows, cols, top, acc):
        part_o[head_rows, cols] = acc[0:16]
        part_ml[h, 0:1, cols] = top
        part_ml[h, 1:2, cols] = acc[16:17]

    attention(keys, vt, 1, 0, keep)

    to_low.wait()
    to_high.wait()
    far_keys[...] = dot(far[...], qkv_w[:, C : 2 * C]).astype(BF)
    far_vt[...] = dot_nt(wt[C : 2 * C], far[...]).astype(BF)

    def merge(h, head_rows, cols, top, acc):
        near_top = part_ml[h, 0:1, cols]
        both = jnp.maximum(near_top, top)
        near, here = jnp.exp(near_top - both), jnp.exp(top - both)
        total = part_ml[h, 1:2, cols] * near + acc[16:17] * here
        att[head_rows, cols] = ((part_o[head_rows, cols] * near + acc[0:16] * here) / total).astype(BF)

    attention(far_keys, far_vt, 0, 1, merge)

    second[...] = (first[...].astype(F32) + dot_tn(att[...], proj_w[...])).astype(BF)


def gelu(x):
    half = 0.5 * x
    return half + half * lax.erf(x * 0.7071067811865476)


def back_kernel(second, aside, mlp_in, mlp_out, out):
    total = second[...].astype(F32)
    normed = (layer_norm(total) * aside[0:1, :]).astype(BF)
    for part in range(4):
        cols = slice(part * 512, (part + 1) * 512)
        hidden = gelu(dot(normed, mlp_in[:, cols])).astype(BF)
        total = total + dot(hidden, mlp_out[cols, :])
    row_id = lax.broadcasted_iota(jnp.int32, (ROWS, C), 0).astype(F32)
    out[0] = jnp.where(row_id < aside[1:2, :], total, 0.0).astype(BF)


def per_device(
    points,
    voxel_index,
    counts,
    cpe_depth,
    cpe_weight,
    cpe_gain,
    norm1_gain,
    qkv_weight,
    proj_weight,
    norm2_gain,
    mlp_in,
    mlp_out,
):
    vmem = pl.BlockSpec(memory_space=pltpu.VMEM)
    hbm = pl.BlockSpec(memory_space=pl.ANY)
    second, aside = pl.pallas_call(
        front_kernel,
        out_shape=(
            jax.ShapeDtypeStruct((ROWS, C), BF),
            jax.ShapeDtypeStruct((8, C), F32),
        ),
        in_specs=[hbm] * 10,
        out_specs=(vmem, vmem),
        scratch_shapes=[
            pltpu.VMEM((ROWS, C), BF),
            pltpu.VMEM((1, ROWS), jnp.int32),
            pltpu.VMEM((1, 1), jnp.int32),
            pltpu.VMEM((27, C), BF),
            pltpu.VMEM((C,), BF),
            pltpu.VMEM((C,), BF),
            pltpu.VMEM((C,), BF),
            pltpu.VMEM((C, C), BF),
            pltpu.VMEM((C, 3 * C), BF),
            pltpu.VMEM((C, C), BF),
            pltpu.VMEM((2 * C, C), BF),
            pltpu.VMEM((VX + 2, VY + 2, VZ, C), BF),
            pltpu.VMEM((27, C), F32),
            pltpu.VMEM((VOX, C), BF),
            pltpu.VMEM((ROWS, C), BF),
            pltpu.VMEM((ROWS, C), BF),
            pltpu.VMEM((ROWS, C), BF),
            pltpu.VMEM((C, ROWS), BF),
            pltpu.VMEM((ROWS, C), BF),
            pltpu.VMEM((C, ROWS), BF),
            pltpu.VMEM((ROWS, C), BF),
            pltpu.VMEM((C, ROWS), BF),
            pltpu.VMEM((2, HALF, 128), BF),
            pltpu.VMEM((128, CQ), BF),
            pltpu.VMEM((2, HALF, ROWS), F32),
            pltpu.VMEM((2, 8, ROWS), F32),
            pltpu.VMEM((C, ROWS), F32),
            pltpu.VMEM((HEADS, 8, ROWS), F32),
            pltpu.VMEM((C, ROWS), BF),
            pltpu.VMEM((8, 128), F32),
            pltpu.VMEM((8, 128), F32),
            pltpu.SemaphoreType.DMA((10,)),
            pltpu.SemaphoreType.DMA((11,)),
            pltpu.SemaphoreType.DMA((11,)),
        ],
        compiler_params=pltpu.CompilerParams(
            collective_id=0, has_side_effects=True, vmem_limit_bytes=48 * 2**20
        ),
        name="front",
    )(
        points,
        voxel_index,
        counts,
        cpe_depth,
        cpe_weight,
        cpe_gain,
        norm1_gain,
        qkv_weight,
        proj_weight,
        norm2_gain,
    )
    return pl.pallas_call(
        back_kernel,
        out_shape=jax.ShapeDtypeStruct((1, ROWS, C), BF),
        in_specs=[vmem] * 4,
        out_specs=vmem,
        compiler_params=pltpu.CompilerParams(vmem_limit_bytes=48 * 2**20),
        name="back",
    )(second, aside, mlp_in, mlp_out)


def solution(mesh):
    in_specs = (P("by", "bx", None), P("by", "bx"), P("by", "bx")) + (P(),) * 9
    return jax.shard_map(
        per_device,
        mesh=mesh,
        in_specs=in_specs,
        out_specs=P("by", "bx", None),
        check_vma=False,
    )
```

```python
import jax
import jax.numpy as jnp
from jax import lax
from jax.experimental import pallas as pl
from jax.experimental.pallas import tpu as pltpu
from jax.sharding import PartitionSpec as P

MESH = pl.DeviceIdType.MESH
BF = jnp.bfloat16
F32 = jnp.float32
C = 512
HEADS = 32
ROWS = 1024
HALF = 512
VX = 8
VY = 16
VZ = 16
VOX = 2048
PLANE = VY * VZ
NEG = -1e30
INNER = (VX - 2) * PLANE
EDGE = 2 * PLANE + (VX - 2) * 2 * VZ
CQ = 256
UNROLL = 4
FRONT_VMEM = 63 * 2**20
BACK_VMEM = 63 * 2**20


def dot(a, b):
    return jnp.dot(a, b, preferred_element_type=F32)


def dot_nt(a, b):
    return lax.dot_general(a, b, (((1,), (1,)), ((), ())), preferred_element_type=F32)


def dot_tn(a, b):
    return lax.dot_general(a, b, (((0,), (0,)), ((), ())), preferred_element_type=F32)


def layer_norm(values):
    center = values - jnp.mean(values, axis=-1, keepdims=True)
    spread = jnp.mean(center * center, axis=-1, keepdims=True)
    return center * lax.rsqrt(spread + 1e-05)


def front_kernel(
    points_hbm,
    voxels_hbm,
    counts_hbm,
    depth_hbm,
    cpe_w_hbm,
    cpe_gain_hbm,
    gain1_hbm,
    qkv_hbm,
    proj_hbm,
    gain2_hbm,
    second,
    aside,
    feats,
    voxels,
    counts,
    depth,
    cpe_gain,
    gain1,
    gain2,
    cpe_w,
    qkv_w,
    proj_w,
    wt,
    grid,
    face_out,
    face_in,
    taps,
    conv,
    edge_sum,
    edge,
    pos,
    first,
    normed,
    far,
    qt,
    keys,
    vt,
    far_keys,
    far_vt,
    bias,
    ones_row,
    scores,
    tops,
    part_o,
    part_ml,
    att,
    count_out,
    count_in,
    load_sem,
    send_sem,
    recv_sem,
):
    bx, by = lax.axis_index("bx"), lax.axis_index("by")
    n_bx, n_by = lax.axis_size("bx"), lax.axis_size("by")
    low_x, high_x = lax.rem(bx + n_bx - 1, n_bx), lax.rem(bx + 1, n_bx)
    low_y, high_y = lax.rem(by + n_by - 1, n_by), lax.rem(by + 1, n_by)

    def at(x, y):
        return {"bx": x, "by": y}

    around = [
        (low_x, by),
        (high_x, by),
        (bx, low_y),
        (bx, high_y),
        (low_x, low_y),
        (low_x, high_y),
        (high_x, low_y),
        (high_x, high_y),
    ]
    barrier = pltpu.get_barrier_semaphore()
    for x, y in around:
        pl.semaphore_signal(barrier, inc=1, device_id=at(x, y), device_id_type=MESH)

    loads = [
        pltpu.make_async_copy(source, held, load_sem.at[i])
        for i, (source, held) in enumerate(
            (
                (voxels_hbm, voxels),
                (counts_hbm, counts),
                (points_hbm.at[0], feats),
                (depth_hbm, depth),
                (cpe_gain_hbm, cpe_gain),
                (gain1_hbm, gain1),
                (gain2_hbm, gain2),
                (cpe_w_hbm, cpe_w),
                (qkv_hbm, qkv_w),
                (proj_hbm, proj_w),
            )
        )
    ]
    for load in loads:
        load.start()

    def remote(i, source, target, where):
        return pltpu.make_async_remote_copy(
            src_ref=source,
            dst_ref=target,
            send_sem=send_sem.at[i],
            recv_sem=recv_sem.at[i],
            device_id=at(*where),
            device_id_type=MESH,
        )

    inner_y = pl.ds(1, VY)
    halo_x = [
        remote(0, grid.at[1, inner_y], grid.at[VX + 1, inner_y], (low_x, by)),
        remote(1, grid.at[VX, inner_y], grid.at[0, inner_y], (high_x, by)),
        remote(2, grid.at[1, 1], grid.at[VX + 1, VY + 1], (low_x, low_y)),
        remote(3, grid.at[1, VY], grid.at[VX + 1, 0], (low_x, high_y)),
        remote(4, grid.at[VX, 1], grid.at[0, VY + 1], (high_x, low_y)),
        remote(5, grid.at[VX, VY], grid.at[0, 0], (high_x, high_y)),
        remote(6, count_out, count_in, (high_x, by)),
    ]
    halo_y = [
        remote(7, face_out.at[0], face_in.at[1], (bx, low_y)),
        remote(8, face_out.at[1], face_in.at[0], (bx, high_y)),
    ]
    low_half, high_half = pl.ds(0, HALF), pl.ds(HALF, HALF)
    to_low = remote(9, normed.at[low_half], far.at[high_half], (low_x, by))
    to_high = remote(10, normed.at[high_half], far.at[low_half], (high_x, by))

    loads[0].wait()
    loads[1].wait()
    count = counts[...].astype(F32)
    count_out[...] = jnp.broadcast_to(count, (8, 128))
    slot = lax.broadcasted_iota(jnp.int32, (1, ROWS), 1)
    where_to = jnp.where(slot.astype(F32) < count, voxels[...], VOX)

    loads[2].wait()

    def scatter(first, second):
        row = lax.broadcasted_iota(jnp.int32, (2 * PLANE, ROWS), 0)
        row = row + jnp.where(row < PLANE, first * PLANE, (second - 1) * PLANE)
        hot = jnp.where(row == where_to, 1.0, 0.0).astype(BF)
        block = dot(hot, feats[...]).astype(BF).reshape(2, VY, VZ, C)
        for i, plane in enumerate((first, second)):
            grid[plane + 1, 1 : VY + 1] = block[i]
            face_out[0, plane] = block[i, 0]
            face_out[1, plane] = block[i, VY - 1]

    scatter(0, VX - 1)
    pl.semaphore_wait(barrier, 8)
    for copy in halo_x:
        copy.start()

    def scatter_step(i, carry):
        scatter(2 * i + 1, 2 * i + 2)
        return carry

    lax.fori_loop(0, VX // 2 - 1, scatter_step, 0)
    for copy in halo_y:
        copy.start()

    loads[3].wait()
    taps[...] = depth[...].astype(F32)

    z = lax.broadcasted_iota(jnp.int32, (VZ, 128), 0)

    def conv_rows(x, end, lanes, y_first, y_count, own):
        parts = [[None] * 3 for _ in range(y_count)]
        for off_x in range(3):
            x_out = off_x - 1 == end and end != 0
            for row in range(y_count + 2):
                y = y_first + row - 1
                y_out = y < 0 or y >= VY
                if own == (x_out or y_out):
                    continue
                if y_out and not x_out:
                    block = face_in[0 if y < 0 else 1, x + off_x - 1, :, lanes].astype(F32)
                else:
                    block = grid[x + off_x, y + 1, :, lanes].astype(F32)
                for i in range(y_count):
                    off_y = row - i
                    if 0 <= off_y <= 2:
                        for off_z in range(3):
                            term = block * taps[pl.ds(9 * off_x + 3 * off_y + off_z, 1), lanes]
                            held = parts[i][off_z]
                            parts[i][off_z] = term if held is None else held + term
        sums = []
        for before, same, after in parts:
            before = jnp.where(z == 0, 0.0, pltpu.roll(before, 1, 0))
            after = jnp.where(z == VZ - 1, 0.0, pltpu.roll(after, VZ - 1, 0))
            sums.append(before + same + after)
        return sums

    def edge_rows(x, end, y):
        if end:
            return pl.ds((0 if end < 0 else PLANE) + y * VZ, VZ)
        start = 2 * PLANE + (x - 1) * 2 * VZ + (0 if y == 0 else VZ)
        return pl.ds(pl.multiple_of(start, VZ), VZ)

    def lane_tile(i):
        return pl.ds(pl.multiple_of(i * 128, 128), 128)

    def inner_step(i, carry):
        lanes = lane_tile(lax.rem(i, 4))
        x = lax.div(i, 4) + 1
        for first_y in range(0, VY, 2):
            for y, total in enumerate(conv_rows(x, 0, lanes, first_y, 2, True), first_y):
                if y in (0, VY - 1):
                    edge_sum[edge_rows(x, 0, y), lanes] = total
                else:
                    start = pl.multiple_of((x - 1) * PLANE + y * VZ, VZ)
                    conv[pl.ds(start, VZ), lanes] = total.astype(BF)
        return carry

    lax.fori_loop(0, 4 * (VX - 2), inner_step, 0)

    def end_step(i, carry):
        lanes = lane_tile(i)
        for x, end in ((0, -1), (VX - 1, 1)):
            for first_y in range(0, VY, 2):
                for y, total in enumerate(conv_rows(x, end, lanes, first_y, 2, True), first_y):
                    edge_sum[edge_rows(x, end, y), lanes] = total
        return carry

    lax.fori_loop(0, 4, end_step, 0)

    for x in range(VX - 2):
        for y in (0, VY - 1):
            conv[x * PLANE + y * VZ : x * PLANE + (y + 1) * VZ] = jnp.zeros((VZ, C), BF)

    def one_hot(index, half, first, size):
        column = jnp.concatenate(
            [
                jnp.broadcast_to(index[:, half * HALF + i * 128 : half * HALF + (i + 1) * 128], (128, 128)).T
                for i in range(HALF // 128)
            ],
            axis=0,
        )
        pieces = [
            jnp.where(
                column == (lax.broadcasted_iota(jnp.int32, (1, 128), 1) + (first + i * 128)).astype(F32),
                1.0,
                0.0,
            ).astype(BF)
            for i in range(size // 128)
        ]
        return jnp.concatenate(pieces, axis=1)

    voxel = voxels[...]
    inner_index = (voxel - PLANE).astype(F32)
    for half in range(2):
        total = None
        for part in range(INNER // HALF):
            hot = one_hot(inner_index, half, part * HALF, HALF)
            term = dot(hot, conv[part * HALF : (part + 1) * HALF])
            total = term if total is None else total + term
        pos[half * HALF : (half + 1) * HALF] = total.astype(BF)

    for load in loads[4:]:
        load.wait()
    wt[0:C] = qkv_w[:, 0:C].T
    wt[C : 2 * C] = qkv_w[:, 2 * C : 3 * C].T

    for copy in halo_x + halo_y:
        copy.wait()
    zero_x = jnp.zeros((VY + 2, VZ, C), BF)
    zero_y = jnp.zeros((VX, VZ, C), BF)
    zero_row = jnp.zeros((VZ, C), BF)

    @pl.when(bx == 0)
    def _():
        grid[0] = zero_x

    @pl.when(bx == n_bx - 1)
    def _():
        grid[VX + 1] = zero_x

    @pl.when(by == 0)
    def _():
        face_in[0] = zero_y
        grid[0, 0] = zero_row
        grid[VX + 1, 0] = zero_row

    @pl.when(by == n_by - 1)
    def _():
        face_in[1] = zero_y
        grid[0, VY + 1] = zero_row
        grid[VX + 1, VY + 1] = zero_row

    def outer_step(i, carry):
        lanes = lane_tile(i)
        for x, end in ((0, -1), (VX - 1, 1)):
            for first_y in range(0, VY, 2):
                for y, total in enumerate(conv_rows(x, end, lanes, first_y, 2, False), first_y):
                    rows = edge_rows(x, end, y)
                    edge[rows, lanes] = (edge_sum[rows, lanes] + total).astype(BF)
        return carry

    lax.fori_loop(0, 4, outer_step, 0)

    def side_step(i, carry):
        lanes = lane_tile(lax.rem(i, 4))
        x = lax.div(i, 4) + 1
        for y in (0, VY - 1):
            rows = edge_rows(x, 0, y)
            total = conv_rows(x, 0, lanes, y, 1, False)[0]
            edge[rows, lanes] = (edge_sum[rows, lanes] + total).astype(BF)
        return carry

    lax.fori_loop(0, 4 * (VX - 2), side_step, 0)

    at_x, at_y = lax.div(voxel, PLANE), lax.rem(lax.div(voxel, VZ), VY)
    at_z = lax.rem(voxel, VZ)
    side = 2 * PLANE + (at_x - 1) * 2 * VZ + at_z
    edge_index = jnp.where(at_y == 0, side, jnp.where(at_y == VY - 1, side + VZ, -1))
    edge_index = jnp.where(at_x == VX - 1, voxel - (VX - 2) * PLANE, edge_index)
    edge_index = jnp.where(at_x == 0, voxel, edge_index).astype(F32)

    def gather(half):
        rows = slice(half * HALF, (half + 1) * HALF)
        total = pos[rows].astype(F32)
        total = total + dot(one_hot(edge_index, half, 0, 512), edge[0:512])
        total = total + dot(one_hot(edge_index, half, 512, 256)[:, : EDGE - 512], edge[512:EDGE])
        branch = layer_norm(dot(total.astype(BF), cpe_w[...])) * cpe_gain[...].reshape(1, C).astype(F32)
        here = (feats[rows].astype(F32) + branch).astype(BF)
        first[rows] = here
        normed[rows] = (layer_norm(here.astype(F32)) * gain1[...].reshape(1, C).astype(F32)).astype(BF)

    gather(0)
    to_low.start()
    gather(1)
    to_high.start()

    qt[...] = (dot_nt(wt[0:C], normed[...]).astype(BF).astype(F32) * 0.25).astype(BF)
    keys[...] = dot(normed[...], qkv_w[:, C : 2 * C]).astype(BF)
    vt[...] = dot_nt(wt[C : 2 * C], normed[...]).astype(BF)

    aside[0:1, :] = gain2[...].reshape(1, C).astype(F32)
    aside[1:2, :] = jnp.broadcast_to(count, (1, C))

    row_id = (lax.broadcasted_iota(jnp.int32, (HALF, 128), 0) + HALF).astype(F32)
    lane_id = lax.broadcasted_iota(jnp.int32, (HALF, 128), 1)
    bias[0] = jnp.where((lane_id == 0) & (row_id >= count), NEG, 0.0).astype(BF)
    bias[1] = jnp.where((lane_id == 0) & (row_id >= count_in[0:1, :]), NEG, 0.0).astype(BF)
    ones_row[...] = jnp.where(
        lax.broadcasted_iota(jnp.int32, (128, CQ), 0) == 0, 1.0, 0.0
    ).astype(BF)

    lane_head = lax.broadcasted_iota(jnp.int32, (1, 128), 1) // 16
    ones16 = jnp.ones((16, HALF), BF)

    def attention(k_ref, v_ref, biased, which, finish):
        def step(h, before, now):
            other = 1 - now
            lanes = pl.ds(pl.multiple_of(lax.div(h, 8) * 128, 128), 128)
            mine = lane_head == lax.rem(h, 8)
            if before is not None:
                head_rows = pl.ds(pl.multiple_of(before * 16, 16), 16)
            for b in range(2):
                rows = slice(b * HALF, (b + 1) * HALF)
                k_h = k_ref[rows, lanes]
                k_h = jnp.where(mine, k_h, jnp.zeros_like(k_h))
                if b == biased:
                    k_h = jnp.concatenate([k_h, bias[which]], axis=1)
                if before is not None:
                    w = jnp.concatenate([v_ref[head_rows, rows], ones16], axis=0)
                for part in range(HALF // CQ):
                    cols = slice(b * HALF + part * CQ, b * HALF + (part + 1) * CQ)
                    q_g = qt[lanes, cols]
                    if b == biased:
                        q_g = jnp.concatenate([q_g, ones_row[...]], axis=0)
                    s = dot(k_h, q_g)
                    scores[now, :, cols] = s
                    tops[now, 0:1, cols] = jnp.max(s, axis=0, keepdims=True)
                    if before is not None:
                        top = tops[other, 0:1, cols]
                        p = jnp.exp(scores[other, :, cols] - top).astype(BF)
                        finish(before, head_rows, cols, top, dot(w, p))

        step(0, None, 0)

        def body(i, carry):
            for u in range(UNROLL):
                before = i * UNROLL + u
                step(jnp.minimum(before + 1, HEADS - 1), before, (u + 1) % 2)
            return carry

        lax.fori_loop(0, HEADS // UNROLL, body, 0)

    def keep(h, head_rows, cols, top, acc):
        part_o[head_rows, cols] = acc[0:16]
        part_ml[h, 0:1, cols] = top
        part_ml[h, 1:2, cols] = acc[16:17]

    attention(keys, vt, 1, 0, keep)

    to_low.wait()
    to_high.wait()
    far_keys[...] = dot(far[...], qkv_w[:, C : 2 * C]).astype(BF)
    far_vt[...] = dot_nt(wt[C : 2 * C], far[...]).astype(BF)

    def merge(h, head_rows, cols, top, acc):
        near_top = part_ml[h, 0:1, cols]
        both = jnp.maximum(near_top, top)
        near, here = jnp.exp(near_top - both), jnp.exp(top - both)
        total = part_ml[h, 1:2, cols] * near + acc[16:17] * here
        att[head_rows, cols] = ((part_o[head_rows, cols] * near + acc[0:16] * here) / total).astype(BF)

    attention(far_keys, far_vt, 0, 1, merge)

    second[...] = (first[...].astype(F32) + dot_tn(att[...], proj_w[...])).astype(BF)


def gelu(x):
    half = 0.5 * x
    return half + half * lax.erf(x * 0.7071067811865476)


def back_kernel(second_hbm, aside_hbm, mlp_in_hbm, mlp_out_hbm, out_hbm, second, aside, mlp_in, mlp_out, out, sem):
    loads = [
        pltpu.make_async_copy(source, held, sem.at[i])
        for i, (source, held) in enumerate(
            (
                (second_hbm, second),
                (aside_hbm, aside),
                (mlp_in_hbm, mlp_in),
                (mlp_out_hbm, mlp_out),
            )
        )
    ]
    for load in loads:
        load.start()
    loads[0].wait()
    loads[1].wait()
    total = second[...].astype(F32)
    normed = (layer_norm(total) * aside[0:1, :]).astype(BF)
    loads[2].wait()
    for part in range(4):
        cols = slice(part * 512, (part + 1) * 512)
        hidden = gelu(dot(normed, mlp_in[:, cols])).astype(BF)
        if part == 0:
            loads[3].wait()
        total = total + dot(hidden, mlp_out[cols, :])
    row_id = lax.broadcasted_iota(jnp.int32, (ROWS, C), 0).astype(F32)
    out[...] = jnp.where(row_id < aside[1:2, :], total, 0.0).astype(BF)
    store = pltpu.make_async_copy(out, out_hbm.at[0], sem.at[4])
    store.start()
    store.wait()


def per_device(
    points,
    voxel_index,
    counts,
    cpe_depth,
    cpe_weight,
    cpe_gain,
    norm1_gain,
    qkv_weight,
    proj_weight,
    norm2_gain,
    mlp_in,
    mlp_out,
):
    vmem = pl.BlockSpec(memory_space=pltpu.VMEM)
    hbm = pl.BlockSpec(memory_space=pl.ANY)
    second, aside = pl.pallas_call(
        front_kernel,
        out_shape=(
            jax.ShapeDtypeStruct((ROWS, C), BF),
            jax.ShapeDtypeStruct((8, C), F32),
        ),
        in_specs=[hbm] * 10,
        out_specs=(vmem, vmem),
        scratch_shapes=[
            pltpu.VMEM((ROWS, C), BF),
            pltpu.VMEM((1, ROWS), jnp.int32),
            pltpu.VMEM((1, 1), jnp.int32),
            pltpu.VMEM((27, C), BF),
            pltpu.VMEM((C,), BF),
            pltpu.VMEM((C,), BF),
            pltpu.VMEM((C,), BF),
            pltpu.VMEM((C, C), BF),
            pltpu.VMEM((C, 3 * C), BF),
            pltpu.VMEM((C, C), BF),
            pltpu.VMEM((2 * C, C), BF),
            pltpu.VMEM((VX + 2, VY + 2, VZ, C), BF),
            pltpu.VMEM((2, VX, VZ, C), BF),
            pltpu.VMEM((2, VX, VZ, C), BF),
            pltpu.VMEM((27, C), F32),
            pltpu.VMEM((INNER, C), BF),
            pltpu.VMEM((EDGE, C), F32),
            pltpu.VMEM((EDGE, C), BF),
            pltpu.VMEM((ROWS, C), BF),
            pltpu.VMEM((ROWS, C), BF),
            pltpu.VMEM((ROWS, C), BF),
            pltpu.VMEM((ROWS, C), BF),
            pltpu.VMEM((C, ROWS), BF),
            pltpu.VMEM((ROWS, C), BF),
            pltpu.VMEM((C, ROWS), BF),
            pltpu.VMEM((ROWS, C), BF),
            pltpu.VMEM((C, ROWS), BF),
            pltpu.VMEM((2, HALF, 128), BF),
            pltpu.VMEM((128, CQ), BF),
            pltpu.VMEM((2, HALF, ROWS), F32),
            pltpu.VMEM((2, 8, ROWS), F32),
            pltpu.VMEM((C, ROWS), F32),
            pltpu.VMEM((HEADS, 8, ROWS), F32),
            pltpu.VMEM((C, ROWS), BF),
            pltpu.VMEM((8, 128), F32),
            pltpu.VMEM((8, 128), F32),
            pltpu.SemaphoreType.DMA((10,)),
            pltpu.SemaphoreType.DMA((11,)),
            pltpu.SemaphoreType.DMA((11,)),
        ],
        compiler_params=pltpu.CompilerParams(
            collective_id=0, has_side_effects=True, vmem_limit_bytes=FRONT_VMEM
        ),
        name="front",
    )(
        points,
        voxel_index,
        counts,
        cpe_depth,
        cpe_weight,
        cpe_gain,
        norm1_gain,
        qkv_weight,
        proj_weight,
        norm2_gain,
    )
    return pl.pallas_call(
        back_kernel,
        out_shape=jax.ShapeDtypeStruct((1, ROWS, C), BF),
        in_specs=[hbm] * 4,
        out_specs=hbm,
        scratch_shapes=[
            pltpu.VMEM((ROWS, C), BF),
            pltpu.VMEM((8, C), F32),
            pltpu.VMEM((C, 4 * C), BF),
            pltpu.VMEM((4 * C, C), BF),
            pltpu.VMEM((ROWS, C), BF),
            pltpu.SemaphoreType.DMA((5,)),
        ],
        compiler_params=pltpu.CompilerParams(vmem_limit_bytes=BACK_VMEM),
        name="back",
    )(second, aside, mlp_in, mlp_out)


def solution(mesh):
    in_specs = (P("by", "bx", None), P("by", "bx"), P("by", "bx")) + (P(),) * 9
    return jax.shard_map(
        per_device,
        mesh=mesh,
        in_specs=in_specs,
        out_specs=P("by", "bx", None),
        check_vma=False,
    )
```

```python
import jax
import jax.numpy as jnp
from jax import lax
from jax.experimental import pallas as pl
from jax.experimental.pallas import tpu as pltpu
from jax.sharding import PartitionSpec as P

MESH = pl.DeviceIdType.MESH
BF = jnp.bfloat16
F32 = jnp.float32
C = 512
HEADS = 32
ROWS = 1024
HALF = 512
VX = 8
VY = 16
VZ = 16
VOX = 2048
PLANE = VY * VZ
NEG = -1e30
INNER = (VX - 2) * PLANE
EDGE = 2 * PLANE + (VX - 2) * 2 * VZ
CQ = 256
UNROLL = 4
FRONT_VMEM = 63 * 2**20
BACK_VMEM = 63 * 2**20


def dot(a, b):
    return jnp.dot(a, b, preferred_element_type=F32)


def dot_nt(a, b):
    return lax.dot_general(a, b, (((1,), (1,)), ((), ())), preferred_element_type=F32)


def dot_tn(a, b):
    return lax.dot_general(a, b, (((0,), (0,)), ((), ())), preferred_element_type=F32)


def layer_norm(values):
    center = values - jnp.mean(values, axis=-1, keepdims=True)
    spread = jnp.mean(center * center, axis=-1, keepdims=True)
    return center * lax.rsqrt(spread + 1e-05)


def front_kernel(
    points_hbm,
    voxels_hbm,
    counts_hbm,
    depth_hbm,
    cpe_w_hbm,
    cpe_gain_hbm,
    gain1_hbm,
    qkv_hbm,
    proj_hbm,
    gain2_hbm,
    second,
    aside,
    feats,
    voxels,
    counts,
    depth,
    cpe_gain,
    gain1,
    gain2,
    cpe_w,
    qkv_w,
    proj_w,
    wt,
    grid,
    face_out,
    face_in,
    taps,
    conv,
    edge_sum,
    edge,
    pos,
    first,
    normed,
    far,
    qt,
    keys,
    vt,
    far_keys,
    far_vt,
    ones,
    scores,
    tops,
    part_o,
    part_ml,
    att,
    count_out,
    count_in,
    load_sem,
    send_sem,
    recv_sem,
):
    bx, by = lax.axis_index("bx"), lax.axis_index("by")
    n_bx, n_by = lax.axis_size("bx"), lax.axis_size("by")
    low_x, high_x = lax.rem(bx + n_bx - 1, n_bx), lax.rem(bx + 1, n_bx)
    low_y, high_y = lax.rem(by + n_by - 1, n_by), lax.rem(by + 1, n_by)

    def at(x, y):
        return {"bx": x, "by": y}

    around = [
        (low_x, by),
        (high_x, by),
        (bx, low_y),
        (bx, high_y),
        (low_x, low_y),
        (low_x, high_y),
        (high_x, low_y),
        (high_x, high_y),
    ]
    barrier = pltpu.get_barrier_semaphore()
    for x, y in around:
        pl.semaphore_signal(barrier, inc=1, device_id=at(x, y), device_id_type=MESH)

    loads = [
        pltpu.make_async_copy(source, held, load_sem.at[i])
        for i, (source, held) in enumerate(
            (
                (voxels_hbm, voxels),
                (counts_hbm, counts),
                (points_hbm.at[0], feats),
                (depth_hbm, depth),
                (cpe_gain_hbm, cpe_gain),
                (gain1_hbm, gain1),
                (gain2_hbm, gain2),
                (cpe_w_hbm, cpe_w),
                (qkv_hbm, qkv_w),
                (proj_hbm, proj_w),
            )
        )
    ]
    for load in loads:
        load.start()

    def remote(i, source, target, where):
        return pltpu.make_async_remote_copy(
            src_ref=source,
            dst_ref=target,
            send_sem=send_sem.at[i],
            recv_sem=recv_sem.at[i],
            device_id=at(*where),
            device_id_type=MESH,
        )

    inner_y = pl.ds(1, VY)
    halo_x = [
        remote(0, grid.at[1, inner_y], grid.at[VX + 1, inner_y], (low_x, by)),
        remote(1, grid.at[VX, inner_y], grid.at[0, inner_y], (high_x, by)),
        remote(2, grid.at[1, 1], grid.at[VX + 1, VY + 1], (low_x, low_y)),
        remote(3, grid.at[1, VY], grid.at[VX + 1, 0], (low_x, high_y)),
        remote(4, grid.at[VX, 1], grid.at[0, VY + 1], (high_x, low_y)),
        remote(5, grid.at[VX, VY], grid.at[0, 0], (high_x, high_y)),
        remote(6, count_out, count_in, (high_x, by)),
    ]
    halo_y = [
        remote(7, face_out.at[0], face_in.at[1], (bx, low_y)),
        remote(8, face_out.at[1], face_in.at[0], (bx, high_y)),
    ]
    low_half, high_half = pl.ds(0, HALF), pl.ds(HALF, HALF)
    to_low = remote(9, normed.at[low_half], far.at[high_half], (low_x, by))
    to_high = remote(10, normed.at[high_half], far.at[low_half], (high_x, by))

    loads[0].wait()
    loads[1].wait()
    count = counts[...].astype(F32)
    count_out[...] = jnp.broadcast_to(count, (8, 128))
    slot = lax.broadcasted_iota(jnp.int32, (1, ROWS), 1)
    where_to = jnp.where(slot.astype(F32) < count, voxels[...], VOX)

    loads[2].wait()

    def scatter(first, second):
        row = lax.broadcasted_iota(jnp.int32, (2 * PLANE, ROWS), 0)
        row = row + jnp.where(row < PLANE, first * PLANE, (second - 1) * PLANE)
        hot = jnp.where(row == where_to, 1.0, 0.0).astype(BF)
        block = dot(hot, feats[...]).astype(BF).reshape(2, VY, VZ, C)
        for i, plane in enumerate((first, second)):
            grid[plane + 1, 1 : VY + 1] = block[i]
            face_out[0, plane] = block[i, 0]
            face_out[1, plane] = block[i, VY - 1]

    scatter(0, VX - 1)
    pl.semaphore_wait(barrier, 8)
    for copy in halo_x:
        copy.start()

    def scatter_step(i, carry):
        scatter(2 * i + 1, 2 * i + 2)
        return carry

    lax.fori_loop(0, VX // 2 - 1, scatter_step, 0)
    for copy in halo_y:
        copy.start()

    loads[3].wait()
    taps[...] = depth[...].astype(F32)

    z = lax.broadcasted_iota(jnp.int32, (VZ, 128), 0)

    def conv_rows(x, end, lanes, y_first, y_count, own):
        parts = [[None] * 3 for _ in range(y_count)]
        for off_x in range(3):
            x_out = off_x - 1 == end and end != 0
            for row in range(y_count + 2):
                y = y_first + row - 1
                y_out = y < 0 or y >= VY
                if own == (x_out or y_out):
                    continue
                if y_out and not x_out:
                    block = face_in[0 if y < 0 else 1, x + off_x - 1, :, lanes].astype(F32)
                else:
                    block = grid[x + off_x, y + 1, :, lanes].astype(F32)
                for i in range(y_count):
                    off_y = row - i
                    if 0 <= off_y <= 2:
                        for off_z in range(3):
                            term = block * taps[pl.ds(9 * off_x + 3 * off_y + off_z, 1), lanes]
                            held = parts[i][off_z]
                            parts[i][off_z] = term if held is None else held + term
        sums = []
        for before, same, after in parts:
            before = jnp.where(z == 0, 0.0, pltpu.roll(before, 1, 0))
            after = jnp.where(z == VZ - 1, 0.0, pltpu.roll(after, VZ - 1, 0))
            sums.append(before + same + after)
        return sums

    def edge_rows(x, end, y):
        if end:
            return pl.ds((0 if end < 0 else PLANE) + y * VZ, VZ)
        start = 2 * PLANE + (x - 1) * 2 * VZ + (0 if y == 0 else VZ)
        return pl.ds(pl.multiple_of(start, VZ), VZ)

    def lane_tile(i):
        return pl.ds(pl.multiple_of(i * 128, 128), 128)

    def inner_step(i, carry):
        lanes = lane_tile(lax.rem(i, 4))
        x = lax.div(i, 4) + 1
        for first_y in range(0, VY, 2):
            for y, total in enumerate(conv_rows(x, 0, lanes, first_y, 2, True), first_y):
                if y in (0, VY - 1):
                    edge_sum[edge_rows(x, 0, y), lanes] = total
                else:
                    start = pl.multiple_of((x - 1) * PLANE + y * VZ, VZ)
                    conv[pl.ds(start, VZ), lanes] = total.astype(BF)
        return carry

    lax.fori_loop(0, 4 * (VX - 2), inner_step, 0)

    def end_step(i, carry):
        lanes = lane_tile(i)
        for x, end in ((0, -1), (VX - 1, 1)):
            for first_y in range(0, VY, 2):
                for y, total in enumerate(conv_rows(x, end, lanes, first_y, 2, True), first_y):
                    edge_sum[edge_rows(x, end, y), lanes] = total
        return carry

    lax.fori_loop(0, 4, end_step, 0)

    for x in range(VX - 2):
        for y in (0, VY - 1):
            conv[x * PLANE + y * VZ : x * PLANE + (y + 1) * VZ] = jnp.zeros((VZ, C), BF)

    def one_hot(index, half, first, size):
        column = jnp.concatenate(
            [
                jnp.broadcast_to(index[:, half * HALF + i * 128 : half * HALF + (i + 1) * 128], (128, 128)).T
                for i in range(HALF // 128)
            ],
            axis=0,
        )
        pieces = [
            jnp.where(
                column == (lax.broadcasted_iota(jnp.int32, (1, 128), 1) + (first + i * 128)).astype(F32),
                1.0,
                0.0,
            ).astype(BF)
            for i in range(size // 128)
        ]
        return jnp.concatenate(pieces, axis=1)

    voxel = voxels[...]
    inner_index = (voxel - PLANE).astype(F32)
    for half in range(2):
        total = None
        for part in range(INNER // HALF):
            hot = one_hot(inner_index, half, part * HALF, HALF)
            term = dot(hot, conv[part * HALF : (part + 1) * HALF])
            total = term if total is None else total + term
        pos[half * HALF : (half + 1) * HALF] = total.astype(BF)

    for load in loads[4:]:
        load.wait()
    wt[0:C] = qkv_w[:, 0:C].T
    wt[C : 2 * C] = qkv_w[:, 2 * C : 3 * C].T

    for copy in halo_x + halo_y:
        copy.wait()
    zero_x = jnp.zeros((VY + 2, VZ, C), BF)
    zero_y = jnp.zeros((VX, VZ, C), BF)
    zero_row = jnp.zeros((VZ, C), BF)

    @pl.when(bx == 0)
    def _():
        grid[0] = zero_x

    @pl.when(bx == n_bx - 1)
    def _():
        grid[VX + 1] = zero_x

    @pl.when(by == 0)
    def _():
        face_in[0] = zero_y
        grid[0, 0] = zero_row
        grid[VX + 1, 0] = zero_row

    @pl.when(by == n_by - 1)
    def _():
        face_in[1] = zero_y
        grid[0, VY + 1] = zero_row
        grid[VX + 1, VY + 1] = zero_row

    def outer_step(i, carry):
        lanes = lane_tile(i)
        for x, end in ((0, -1), (VX - 1, 1)):
            for first_y in range(0, VY, 2):
                for y, total in enumerate(conv_rows(x, end, lanes, first_y, 2, False), first_y):
                    rows = edge_rows(x, end, y)
                    edge[rows, lanes] = (edge_sum[rows, lanes] + total).astype(BF)
        return carry

    lax.fori_loop(0, 4, outer_step, 0)

    def side_step(i, carry):
        lanes = lane_tile(lax.rem(i, 4))
        x = lax.div(i, 4) + 1
        for y in (0, VY - 1):
            rows = edge_rows(x, 0, y)
            total = conv_rows(x, 0, lanes, y, 1, False)[0]
            edge[rows, lanes] = (edge_sum[rows, lanes] + total).astype(BF)
        return carry

    lax.fori_loop(0, 4 * (VX - 2), side_step, 0)

    at_x, at_y = lax.div(voxel, PLANE), lax.rem(lax.div(voxel, VZ), VY)
    at_z = lax.rem(voxel, VZ)
    side = 2 * PLANE + (at_x - 1) * 2 * VZ + at_z
    edge_index = jnp.where(at_y == 0, side, jnp.where(at_y == VY - 1, side + VZ, -1))
    edge_index = jnp.where(at_x == VX - 1, voxel - (VX - 2) * PLANE, edge_index)
    edge_index = jnp.where(at_x == 0, voxel, edge_index).astype(F32)

    def gather(half):
        rows = slice(half * HALF, (half + 1) * HALF)
        total = pos[rows].astype(F32)
        total = total + dot(one_hot(edge_index, half, 0, 512), edge[0:512])
        total = total + dot(one_hot(edge_index, half, 512, 256)[:, : EDGE - 512], edge[512:EDGE])
        branch = layer_norm(dot(total.astype(BF), cpe_w[...])) * cpe_gain[...].reshape(1, C).astype(F32)
        here = (feats[rows].astype(F32) + branch).astype(BF)
        first[rows] = here
        normed[rows] = (layer_norm(here.astype(F32)) * gain1[...].reshape(1, C).astype(F32)).astype(BF)

    gather(0)
    to_low.start()
    gather(1)
    to_high.start()

    qt[...] = (dot_nt(wt[0:C], normed[...]).astype(BF).astype(F32) * 0.25).astype(BF)
    keys[...] = dot(normed[...], qkv_w[:, C : 2 * C]).astype(BF)
    vt[...] = dot_nt(wt[C : 2 * C], normed[...]).astype(BF)

    aside[0:1, :] = gain2[...].reshape(1, C).astype(F32)
    aside[1:2, :] = jnp.broadcast_to(count, (1, C))

    row_id = (lax.broadcasted_iota(jnp.int32, (HALF, 1), 0) + HALF).astype(F32)
    col_id = (lax.broadcasted_iota(jnp.int32, (1, HALF), 1) + HALF).astype(F32)

    def drop_invalid(k_ref, v_ref, start, total, which):
        here = slice(start, start + HALF)
        held = k_ref[here].astype(F32)
        k_ref[here] = jnp.where(row_id < total, held, held[0:1]).astype(BF)
        v_ref[:, here] = jnp.where(col_id < total, v_ref[:, here].astype(F32), 0.0).astype(BF)
        ones[which] = jnp.broadcast_to(jnp.where(col_id < total, 1.0, 0.0), (16, HALF)).astype(BF)

    drop_invalid(keys, vt, HALF, count, 0)

    lane_head = lax.broadcasted_iota(jnp.int32, (1, 128), 1) // 16
    all_ones = jnp.ones((16, HALF), BF)

    def attention(k_ref, v_ref, partial, which, finish):
        def step(h, before, now):
            other = 1 - now
            lanes = pl.ds(pl.multiple_of(lax.div(h, 8) * 128, 128), 128)
            mine = lane_head == lax.rem(h, 8)
            if before is not None:
                head_rows = pl.ds(pl.multiple_of(before * 16, 16), 16)
            for b in range(2):
                rows = slice(b * HALF, (b + 1) * HALF)
                k_h = k_ref[rows, lanes]
                k_h = jnp.where(mine, k_h, jnp.zeros_like(k_h))
                if before is not None:
                    counted = ones[which] if b == partial else all_ones
                    w = jnp.concatenate([v_ref[head_rows, rows], counted], axis=0)
                for part in range(HALF // CQ):
                    cols = slice(b * HALF + part * CQ, b * HALF + (part + 1) * CQ)
                    q_g = qt[lanes, cols]
                    s = dot(k_h, q_g)
                    scores[now, :, cols] = s
                    tops[now, 0:1, cols] = jnp.max(s, axis=0, keepdims=True)
                    if before is not None:
                        top = tops[other, 0:1, cols]
                        p = jnp.exp(scores[other, :, cols] - top).astype(BF)
                        finish(before, head_rows, cols, top, dot(w, p))

        step(0, None, 0)

        def body(i, carry):
            for u in range(UNROLL):
                before = i * UNROLL + u
                step(jnp.minimum(before + 1, HEADS - 1), before, (u + 1) % 2)
            return carry

        lax.fori_loop(0, HEADS // UNROLL, body, 0)

    def keep(h, head_rows, cols, top, acc):
        part_o[head_rows, cols] = acc[0:16]
        part_ml[h, 0:1, cols] = top
        part_ml[h, 1:2, cols] = acc[16:17]

    attention(keys, vt, 1, 0, keep)

    to_low.wait()
    to_high.wait()
    far_keys[...] = dot(far[...], qkv_w[:, C : 2 * C]).astype(BF)
    far_vt[...] = dot_nt(wt[C : 2 * C], far[...]).astype(BF)
    drop_invalid(far_keys, far_vt, 0, count_in[0:1, 0:1], 1)

    def merge(h, head_rows, cols, top, acc):
        near_top = part_ml[h, 0:1, cols]
        both = jnp.maximum(near_top, top)
        near, here = jnp.exp(near_top - both), jnp.exp(top - both)
        total = part_ml[h, 1:2, cols] * near + acc[16:17] * here
        att[head_rows, cols] = ((part_o[head_rows, cols] * near + acc[0:16] * here) / total).astype(BF)

    attention(far_keys, far_vt, 0, 1, merge)

    second[...] = (first[...].astype(F32) + dot_tn(att[...], proj_w[...])).astype(BF)


def gelu(x):
    half = 0.5 * x
    return half + half * lax.erf(x * 0.7071067811865476)


def back_kernel(second_hbm, aside_hbm, mlp_in_hbm, mlp_out_hbm, out_hbm, second, aside, mlp_in, mlp_out, out, sem):
    loads = [
        pltpu.make_async_copy(source, held, sem.at[i])
        for i, (source, held) in enumerate(
            (
                (second_hbm, second),
                (aside_hbm, aside),
                (mlp_in_hbm, mlp_in),
                (mlp_out_hbm, mlp_out),
            )
        )
    ]
    for load in loads:
        load.start()
    loads[0].wait()
    loads[1].wait()
    total = second[...].astype(F32)
    normed = (layer_norm(total) * aside[0:1, :]).astype(BF)
    loads[2].wait()
    for part in range(4):
        cols = slice(part * 512, (part + 1) * 512)
        hidden = gelu(dot(normed, mlp_in[:, cols])).astype(BF)
        if part == 0:
            loads[3].wait()
        total = total + dot(hidden, mlp_out[cols, :])
    row_id = lax.broadcasted_iota(jnp.int32, (ROWS, C), 0).astype(F32)
    out[...] = jnp.where(row_id < aside[1:2, :], total, 0.0).astype(BF)
    store = pltpu.make_async_copy(out, out_hbm.at[0], sem.at[4])
    store.start()
    store.wait()


def per_device(
    points,
    voxel_index,
    counts,
    cpe_depth,
    cpe_weight,
    cpe_gain,
    norm1_gain,
    qkv_weight,
    proj_weight,
    norm2_gain,
    mlp_in,
    mlp_out,
):
    vmem = pl.BlockSpec(memory_space=pltpu.VMEM)
    hbm = pl.BlockSpec(memory_space=pl.ANY)
    second, aside = pl.pallas_call(
        front_kernel,
        out_shape=(
            jax.ShapeDtypeStruct((ROWS, C), BF),
            jax.ShapeDtypeStruct((8, C), F32),
        ),
        in_specs=[hbm] * 10,
        out_specs=(vmem, vmem),
        scratch_shapes=[
            pltpu.VMEM((ROWS, C), BF),
            pltpu.VMEM((1, ROWS), jnp.int32),
            pltpu.VMEM((1, 1), jnp.int32),
            pltpu.VMEM((27, C), BF),
            pltpu.VMEM((C,), BF),
            pltpu.VMEM((C,), BF),
            pltpu.VMEM((C,), BF),
            pltpu.VMEM((C, C), BF),
            pltpu.VMEM((C, 3 * C), BF),
            pltpu.VMEM((C, C), BF),
            pltpu.VMEM((2 * C, C), BF),
            pltpu.VMEM((VX + 2, VY + 2, VZ, C), BF),
            pltpu.VMEM((2, VX, VZ, C), BF),
            pltpu.VMEM((2, VX, VZ, C), BF),
            pltpu.VMEM((27, C), F32),
            pltpu.VMEM((INNER, C), BF),
            pltpu.VMEM((EDGE, C), F32),
            pltpu.VMEM((EDGE, C), BF),
            pltpu.VMEM((ROWS, C), BF),
            pltpu.VMEM((ROWS, C), BF),
            pltpu.VMEM((ROWS, C), BF),
            pltpu.VMEM((ROWS, C), BF),
            pltpu.VMEM((C, ROWS), BF),
            pltpu.VMEM((ROWS, C), BF),
            pltpu.VMEM((C, ROWS), BF),
            pltpu.VMEM((ROWS, C), BF),
            pltpu.VMEM((C, ROWS), BF),
            pltpu.VMEM((2, 16, HALF), BF),
            pltpu.VMEM((2, HALF, ROWS), F32),
            pltpu.VMEM((2, 8, ROWS), F32),
            pltpu.VMEM((C, ROWS), F32),
            pltpu.VMEM((HEADS, 8, ROWS), F32),
            pltpu.VMEM((C, ROWS), BF),
            pltpu.VMEM((8, 128), F32),
            pltpu.VMEM((8, 128), F32),
            pltpu.SemaphoreType.DMA((10,)),
            pltpu.SemaphoreType.DMA((11,)),
            pltpu.SemaphoreType.DMA((11,)),
        ],
        compiler_params=pltpu.CompilerParams(
            collective_id=0, has_side_effects=True, vmem_limit_bytes=FRONT_VMEM
        ),
        name="front",
    )(
        points,
        voxel_index,
        counts,
        cpe_depth,
        cpe_weight,
        cpe_gain,
        norm1_gain,
        qkv_weight,
        proj_weight,
        norm2_gain,
    )
    return pl.pallas_call(
        back_kernel,
        out_shape=jax.ShapeDtypeStruct((1, ROWS, C), BF),
        in_specs=[hbm] * 4,
        out_specs=hbm,
        scratch_shapes=[
            pltpu.VMEM((ROWS, C), BF),
            pltpu.VMEM((8, C), F32),
            pltpu.VMEM((C, 4 * C), BF),
            pltpu.VMEM((4 * C, C), BF),
            pltpu.VMEM((ROWS, C), BF),
            pltpu.SemaphoreType.DMA((5,)),
        ],
        compiler_params=pltpu.CompilerParams(vmem_limit_bytes=BACK_VMEM),
        name="back",
    )(second, aside, mlp_in, mlp_out)


def solution(mesh):
    in_specs = (P("by", "bx", None), P("by", "bx"), P("by", "bx")) + (P(),) * 9
    return jax.shard_map(
        per_device,
        mesh=mesh,
        in_specs=in_specs,
        out_specs=P("by", "bx", None),
        check_vma=False,
    )
```

```python
import jax
import jax.numpy as jnp
from jax import lax
from jax.experimental import pallas as pl
from jax.experimental.pallas import tpu as pltpu
from jax.sharding import PartitionSpec as P

MESH = pl.DeviceIdType.MESH
BF = jnp.bfloat16
F32 = jnp.float32
C = 512
HEADS = 32
ROWS = 1024
HALF = 512
VX = 8
VY = 16
VZ = 16
VOX = 2048
PLANE = VY * VZ
NEG = -1e30
INNER = (VX - 2) * PLANE
EDGE = 2 * PLANE + (VX - 2) * 2 * VZ
CQ = 256
UNROLL = 4
FRONT_VMEM = 63 * 2**20
BACK_VMEM = 63 * 2**20


def dot(a, b):
    return jnp.dot(a, b, preferred_element_type=F32)


def dot_nt(a, b):
    return lax.dot_general(a, b, (((1,), (1,)), ((), ())), preferred_element_type=F32)


def dot_tn(a, b):
    return lax.dot_general(a, b, (((0,), (0,)), ((), ())), preferred_element_type=F32)


def layer_norm(values):
    center = values - jnp.mean(values, axis=-1, keepdims=True)
    spread = jnp.mean(center * center, axis=-1, keepdims=True)
    return center * lax.rsqrt(spread + 1e-05)


def front_kernel(
    points_hbm,
    voxels_hbm,
    counts_hbm,
    depth_hbm,
    cpe_w_hbm,
    cpe_gain_hbm,
    gain1_hbm,
    qkv_hbm,
    proj_hbm,
    gain2_hbm,
    second,
    aside,
    feats,
    voxels,
    counts,
    depth,
    cpe_gain,
    gain1,
    gain2,
    cpe_w,
    qkv_w,
    proj_w,
    wt,
    grid,
    face_out,
    face_in,
    taps,
    conv,
    edge_sum,
    edge,
    pos,
    first,
    normed,
    far,
    qt,
    keys,
    vt,
    far_keys,
    far_vt,
    ones,
    scores,
    tops,
    part_o,
    part_ml,
    att,
    count_out,
    count_in,
    load_sem,
    send_sem,
    recv_sem,
):
    bx, by = lax.axis_index("bx"), lax.axis_index("by")
    n_bx, n_by = lax.axis_size("bx"), lax.axis_size("by")
    low_x, high_x = lax.rem(bx + n_bx - 1, n_bx), lax.rem(bx + 1, n_bx)
    low_y, high_y = lax.rem(by + n_by - 1, n_by), lax.rem(by + 1, n_by)

    def at(x, y):
        return {"bx": x, "by": y}

    around = [
        (low_x, by),
        (high_x, by),
        (bx, low_y),
        (bx, high_y),
        (low_x, low_y),
        (low_x, high_y),
        (high_x, low_y),
        (high_x, high_y),
    ]
    barrier = pltpu.get_barrier_semaphore()
    for x, y in around:
        pl.semaphore_signal(barrier, inc=1, device_id=at(x, y), device_id_type=MESH)

    loads = [
        pltpu.make_async_copy(source, held, load_sem.at[i])
        for i, (source, held) in enumerate(
            (
                (voxels_hbm, voxels),
                (counts_hbm, counts),
                (points_hbm.at[0], feats),
                (depth_hbm, depth),
                (cpe_gain_hbm, cpe_gain),
                (gain1_hbm, gain1),
                (gain2_hbm, gain2),
                (cpe_w_hbm, cpe_w),
                (qkv_hbm, qkv_w),
                (proj_hbm, proj_w),
            )
        )
    ]
    for load in loads[:7]:
        load.start()

    def remote(i, source, target, where):
        return pltpu.make_async_remote_copy(
            src_ref=source,
            dst_ref=target,
            send_sem=send_sem.at[i],
            recv_sem=recv_sem.at[i],
            device_id=at(*where),
            device_id_type=MESH,
        )

    inner_y = pl.ds(1, VY)
    halo_x = [
        remote(0, grid.at[1, inner_y], grid.at[VX + 1, inner_y], (low_x, by)),
        remote(1, grid.at[VX, inner_y], grid.at[0, inner_y], (high_x, by)),
        remote(2, grid.at[1, 1], grid.at[VX + 1, VY + 1], (low_x, low_y)),
        remote(3, grid.at[1, VY], grid.at[VX + 1, 0], (low_x, high_y)),
        remote(4, grid.at[VX, 1], grid.at[0, VY + 1], (high_x, low_y)),
        remote(5, grid.at[VX, VY], grid.at[0, 0], (high_x, high_y)),
        remote(6, count_out, count_in, (high_x, by)),
    ]
    halo_y = [
        remote(7, face_out.at[0], face_in.at[1], (bx, low_y)),
        remote(8, face_out.at[1], face_in.at[0], (bx, high_y)),
    ]
    low_half, high_half = pl.ds(0, HALF), pl.ds(HALF, HALF)
    to_low = remote(9, normed.at[low_half], far.at[high_half], (low_x, by))
    to_high = remote(10, normed.at[high_half], far.at[low_half], (high_x, by))

    loads[0].wait()
    loads[1].wait()
    count = counts[...].astype(F32)
    count_out[...] = jnp.broadcast_to(count, (8, 128))
    slot = lax.broadcasted_iota(jnp.int32, (1, ROWS), 1)
    where_to = jnp.where(slot.astype(F32) < count, voxels[...], VOX)

    loads[2].wait()
    for load in loads[7:]:
        load.start()

    def scatter(first, second):
        row = lax.broadcasted_iota(jnp.int32, (2 * PLANE, ROWS), 0)
        row = row + jnp.where(row < PLANE, first * PLANE, (second - 1) * PLANE)
        hot = jnp.where(row == where_to, 1.0, 0.0).astype(BF)
        block = dot(hot, feats[...]).astype(BF).reshape(2, VY, VZ, C)
        for i, plane in enumerate((first, second)):
            grid[plane + 1, 1 : VY + 1] = block[i]
        return block

    ends = scatter(0, VX - 1)
    pl.semaphore_wait(barrier, 8)
    for copy in halo_x:
        copy.start()

    face = lax.broadcasted_iota(jnp.int32, ((VX - 2) * 2 * VZ, ROWS), 0)
    in_plane = lax.rem(face, 2 * VZ)
    face = PLANE + lax.div(face, 2 * VZ) * PLANE + in_plane
    face = face + jnp.where(in_plane < VZ, 0, PLANE - 2 * VZ)
    hot = jnp.where(face == where_to, 1.0, 0.0).astype(BF)
    sides = dot(hot, feats[...]).astype(BF).reshape(VX - 2, 2, VZ, C)
    for i in range(2):
        face_out[i, 1 : VX - 1] = sides[:, i]
        face_out[i, 0] = ends[0, i * (VY - 1)]
        face_out[i, VX - 1] = ends[1, i * (VY - 1)]
    for copy in halo_y:
        copy.start()

    def scatter_step(i, carry):
        scatter(2 * i + 1, 2 * i + 2)
        return carry

    lax.fori_loop(0, VX // 2 - 1, scatter_step, 0)

    loads[3].wait()
    taps[...] = depth[...].astype(F32)

    z = lax.broadcasted_iota(jnp.int32, (VZ, 128), 0)

    def conv_rows(x, end, lanes, y_first, y_count, own):
        parts = [[None] * 3 for _ in range(y_count)]
        for off_x in range(3):
            x_out = off_x - 1 == end and end != 0
            for row in range(y_count + 2):
                y = y_first + row - 1
                y_out = y < 0 or y >= VY
                if own == (x_out or y_out):
                    continue
                if y_out and not x_out:
                    block = face_in[0 if y < 0 else 1, x + off_x - 1, :, lanes].astype(F32)
                else:
                    block = grid[x + off_x, y + 1, :, lanes].astype(F32)
                for i in range(y_count):
                    off_y = row - i
                    if 0 <= off_y <= 2:
                        for off_z in range(3):
                            term = block * taps[pl.ds(9 * off_x + 3 * off_y + off_z, 1), lanes]
                            held = parts[i][off_z]
                            parts[i][off_z] = term if held is None else held + term
        sums = []
        for before, same, after in parts:
            before = jnp.where(z == 0, 0.0, pltpu.roll(before, 1, 0))
            after = jnp.where(z == VZ - 1, 0.0, pltpu.roll(after, VZ - 1, 0))
            sums.append(before + same + after)
        return sums

    def edge_rows(x, end, y):
        if end:
            return pl.ds((0 if end < 0 else PLANE) + y * VZ, VZ)
        start = 2 * PLANE + (x - 1) * 2 * VZ + (0 if y == 0 else VZ)
        return pl.ds(pl.multiple_of(start, VZ), VZ)

    def lane_tile(i):
        return pl.ds(pl.multiple_of(i * 128, 128), 128)

    def inner_step(i, carry):
        lanes = lane_tile(lax.rem(i, 4))
        x = lax.div(i, 4) + 1
        for first_y in range(0, VY, 2):
            for y, total in enumerate(conv_rows(x, 0, lanes, first_y, 2, True), first_y):
                if y in (0, VY - 1):
                    edge_sum[edge_rows(x, 0, y), lanes] = total
                else:
                    start = pl.multiple_of((x - 1) * PLANE + y * VZ, VZ)
                    conv[pl.ds(start, VZ), lanes] = total.astype(BF)
        return carry

    lax.fori_loop(0, 4 * (VX - 2), inner_step, 0)

    def end_step(i, carry):
        lanes = lane_tile(i)
        for x, end in ((0, -1), (VX - 1, 1)):
            for first_y in range(0, VY, 2):
                for y, total in enumerate(conv_rows(x, end, lanes, first_y, 2, True), first_y):
                    edge_sum[edge_rows(x, end, y), lanes] = total
        return carry

    lax.fori_loop(0, 4, end_step, 0)

    for x in range(VX - 2):
        for y in (0, VY - 1):
            conv[x * PLANE + y * VZ : x * PLANE + (y + 1) * VZ] = jnp.zeros((VZ, C), BF)

    def one_hot(index, half, first, size):
        column = jnp.concatenate(
            [
                jnp.broadcast_to(index[:, half * HALF + i * 128 : half * HALF + (i + 1) * 128], (128, 128)).T
                for i in range(HALF // 128)
            ],
            axis=0,
        )
        pieces = [
            jnp.where(
                column == (lax.broadcasted_iota(jnp.int32, (1, 128), 1) + (first + i * 128)).astype(F32),
                1.0,
                0.0,
            ).astype(BF)
            for i in range(size // 128)
        ]
        return jnp.concatenate(pieces, axis=1)

    voxel = voxels[...]
    inner_index = (voxel - PLANE).astype(F32)
    for half in range(2):
        total = None
        for part in range(INNER // HALF):
            hot = one_hot(inner_index, half, part * HALF, HALF)
            term = dot(hot, conv[part * HALF : (part + 1) * HALF])
            total = term if total is None else total + term
        pos[half * HALF : (half + 1) * HALF] = total.astype(BF)

    for load in loads[4:]:
        load.wait()
    wt[0:C] = qkv_w[:, 0:C].T
    wt[C : 2 * C] = qkv_w[:, 2 * C : 3 * C].T

    for copy in halo_x + halo_y:
        copy.wait()
    zero_x = jnp.zeros((VY + 2, VZ, C), BF)
    zero_y = jnp.zeros((VX, VZ, C), BF)
    zero_row = jnp.zeros((VZ, C), BF)

    @pl.when(bx == 0)
    def _():
        grid[0] = zero_x

    @pl.when(bx == n_bx - 1)
    def _():
        grid[VX + 1] = zero_x

    @pl.when(by == 0)
    def _():
        face_in[0] = zero_y
        grid[0, 0] = zero_row
        grid[VX + 1, 0] = zero_row

    @pl.when(by == n_by - 1)
    def _():
        face_in[1] = zero_y
        grid[0, VY + 1] = zero_row
        grid[VX + 1, VY + 1] = zero_row

    def outer_step(i, carry):
        lanes = lane_tile(i)
        for x, end in ((0, -1), (VX - 1, 1)):
            for first_y in range(0, VY, 2):
                for y, total in enumerate(conv_rows(x, end, lanes, first_y, 2, False), first_y):
                    rows = edge_rows(x, end, y)
                    edge[rows, lanes] = (edge_sum[rows, lanes] + total).astype(BF)
        return carry

    lax.fori_loop(0, 4, outer_step, 0)

    def side_step(i, carry):
        lanes = lane_tile(lax.rem(i, 4))
        x = lax.div(i, 4) + 1
        for y in (0, VY - 1):
            rows = edge_rows(x, 0, y)
            total = conv_rows(x, 0, lanes, y, 1, False)[0]
            edge[rows, lanes] = (edge_sum[rows, lanes] + total).astype(BF)
        return carry

    lax.fori_loop(0, 4 * (VX - 2), side_step, 0)

    at_x, at_y = lax.div(voxel, PLANE), lax.rem(lax.div(voxel, VZ), VY)
    at_z = lax.rem(voxel, VZ)
    side = 2 * PLANE + (at_x - 1) * 2 * VZ + at_z
    edge_index = jnp.where(at_y == 0, side, jnp.where(at_y == VY - 1, side + VZ, -1))
    edge_index = jnp.where(at_x == VX - 1, voxel - (VX - 2) * PLANE, edge_index)
    edge_index = jnp.where(at_x == 0, voxel, edge_index).astype(F32)

    def gather(half):
        rows = slice(half * HALF, (half + 1) * HALF)
        total = pos[rows].astype(F32)
        total = total + dot(one_hot(edge_index, half, 0, 512), edge[0:512])
        total = total + dot(one_hot(edge_index, half, 512, 256)[:, : EDGE - 512], edge[512:EDGE])
        branch = layer_norm(dot(total.astype(BF), cpe_w[...])) * cpe_gain[...].reshape(1, C).astype(F32)
        here = (feats[rows].astype(F32) + branch).astype(BF)
        first[rows] = here
        normed[rows] = (layer_norm(here.astype(F32)) * gain1[...].reshape(1, C).astype(F32)).astype(BF)

    gather(0)
    to_low.start()
    gather(1)
    to_high.start()

    qt[...] = (dot_nt(wt[0:C], normed[...]).astype(BF).astype(F32) * 0.25).astype(BF)
    keys[...] = dot(normed[...], qkv_w[:, C : 2 * C]).astype(BF)
    vt[...] = dot_nt(wt[C : 2 * C], normed[...]).astype(BF)

    aside[0:1, :] = gain2[...].reshape(1, C).astype(F32)
    aside[1:2, :] = jnp.broadcast_to(count, (1, C))

    row_id = (lax.broadcasted_iota(jnp.int32, (HALF, 1), 0) + HALF).astype(F32)
    col_id = (lax.broadcasted_iota(jnp.int32, (1, HALF), 1) + HALF).astype(F32)

    def drop_invalid(k_ref, v_ref, start, total, which):
        here = slice(start, start + HALF)
        held = k_ref[here].astype(F32)
        k_ref[here] = jnp.where(row_id < total, held, held[0:1]).astype(BF)
        v_ref[:, here] = jnp.where(col_id < total, v_ref[:, here].astype(F32), 0.0).astype(BF)
        ones[which] = jnp.broadcast_to(jnp.where(col_id < total, 1.0, 0.0), (16, HALF)).astype(BF)

    drop_invalid(keys, vt, HALF, count, 0)

    lane_head = lax.broadcasted_iota(jnp.int32, (1, 128), 1) // 16
    all_ones = jnp.ones((16, HALF), BF)

    def attention(k_ref, v_ref, partial, which, finish):
        def step(h, before, now):
            other = 1 - now
            lanes = pl.ds(pl.multiple_of(lax.div(h, 8) * 128, 128), 128)
            mine = lane_head == lax.rem(h, 8)
            if before is not None:
                head_rows = pl.ds(pl.multiple_of(before * 16, 16), 16)
            for b in range(2):
                rows = slice(b * HALF, (b + 1) * HALF)
                k_h = k_ref[rows, lanes]
                k_h = jnp.where(mine, k_h, jnp.zeros_like(k_h))
                if before is not None:
                    counted = ones[which] if b == partial else all_ones
                    w = jnp.concatenate([v_ref[head_rows, rows], counted], axis=0)
                for part in range(HALF // CQ):
                    cols = slice(b * HALF + part * CQ, b * HALF + (part + 1) * CQ)
                    q_g = qt[lanes, cols]
                    s = dot(k_h, q_g)
                    scores[now, :, cols] = s
                    tops[now, 0:1, cols] = jnp.max(s, axis=0, keepdims=True)
                    if before is not None:
                        top = tops[other, 0:1, cols]
                        p = jnp.exp(scores[other, :, cols] - top).astype(BF)
                        finish(before, head_rows, cols, top, dot(w, p))

        step(0, None, 0)

        def body(i, carry):
            for u in range(UNROLL):
                before = i * UNROLL + u
                step(jnp.minimum(before + 1, HEADS - 1), before, (u + 1) % 2)
            return carry

        lax.fori_loop(0, HEADS // UNROLL, body, 0)

    def keep(h, head_rows, cols, top, acc):
        part_o[head_rows, cols] = acc[0:16]
        part_ml[h, 0:1, cols] = top
        part_ml[h, 1:2, cols] = acc[16:17]

    attention(keys, vt, 1, 0, keep)

    to_low.wait()
    to_high.wait()
    far_keys[...] = dot(far[...], qkv_w[:, C : 2 * C]).astype(BF)
    far_vt[...] = dot_nt(wt[C : 2 * C], far[...]).astype(BF)
    drop_invalid(far_keys, far_vt, 0, count_in[0:1, 0:1], 1)

    def merge(h, head_rows, cols, top, acc):
        near_top = part_ml[h, 0:1, cols]
        both = jnp.maximum(near_top, top)
        near, here = jnp.exp(near_top - both), jnp.exp(top - both)
        total = part_ml[h, 1:2, cols] * near + acc[16:17] * here
        att[head_rows, cols] = ((part_o[head_rows, cols] * near + acc[0:16] * here) / total).astype(BF)

    attention(far_keys, far_vt, 0, 1, merge)

    second[...] = (first[...].astype(F32) + dot_tn(att[...], proj_w[...])).astype(BF)


def gelu(x):
    half = 0.5 * x
    return half + half * lax.erf(x * 0.7071067811865476)


def back_kernel(second_hbm, aside_hbm, mlp_in_hbm, mlp_out_hbm, out_hbm, second, aside, mlp_in, mlp_out, out, sem):
    loads = [
        pltpu.make_async_copy(source, held, sem.at[i])
        for i, (source, held) in enumerate(
            (
                (second_hbm, second),
                (aside_hbm, aside),
                (mlp_in_hbm, mlp_in),
                (mlp_out_hbm, mlp_out),
            )
        )
    ]
    for load in loads:
        load.start()
    loads[0].wait()
    loads[1].wait()
    total = second[...].astype(F32)
    normed = (layer_norm(total) * aside[0:1, :]).astype(BF)
    loads[2].wait()
    for part in range(4):
        cols = slice(part * 512, (part + 1) * 512)
        hidden = gelu(dot(normed, mlp_in[:, cols])).astype(BF)
        if part == 0:
            loads[3].wait()
        total = total + dot(hidden, mlp_out[cols, :])
    row_id = lax.broadcasted_iota(jnp.int32, (ROWS, C), 0).astype(F32)
    out[...] = jnp.where(row_id < aside[1:2, :], total, 0.0).astype(BF)
    store = pltpu.make_async_copy(out, out_hbm.at[0], sem.at[4])
    store.start()
    store.wait()


def per_device(
    points,
    voxel_index,
    counts,
    cpe_depth,
    cpe_weight,
    cpe_gain,
    norm1_gain,
    qkv_weight,
    proj_weight,
    norm2_gain,
    mlp_in,
    mlp_out,
):
    vmem = pl.BlockSpec(memory_space=pltpu.VMEM)
    hbm = pl.BlockSpec(memory_space=pl.ANY)
    second, aside = pl.pallas_call(
        front_kernel,
        out_shape=(
            jax.ShapeDtypeStruct((ROWS, C), BF),
            jax.ShapeDtypeStruct((8, C), F32),
        ),
        in_specs=[hbm] * 10,
        out_specs=(vmem, vmem),
        scratch_shapes=[
            pltpu.VMEM((ROWS, C), BF),
            pltpu.VMEM((1, ROWS), jnp.int32),
            pltpu.VMEM((1, 1), jnp.int32),
            pltpu.VMEM((27, C), BF),
            pltpu.VMEM((C,), BF),
            pltpu.VMEM((C,), BF),
            pltpu.VMEM((C,), BF),
            pltpu.VMEM((C, C), BF),
            pltpu.VMEM((C, 3 * C), BF),
            pltpu.VMEM((C, C), BF),
            pltpu.VMEM((2 * C, C), BF),
            pltpu.VMEM((VX + 2, VY + 2, VZ, C), BF),
            pltpu.VMEM((2, VX, VZ, C), BF),
            pltpu.VMEM((2, VX, VZ, C), BF),
            pltpu.VMEM((27, C), F32),
            pltpu.VMEM((INNER, C), BF),
            pltpu.VMEM((EDGE, C), F32),
            pltpu.VMEM((EDGE, C), BF),
            pltpu.VMEM((ROWS, C), BF),
            pltpu.VMEM((ROWS, C), BF),
            pltpu.VMEM((ROWS, C), BF),
            pltpu.VMEM((ROWS, C), BF),
            pltpu.VMEM((C, ROWS), BF),
            pltpu.VMEM((ROWS, C), BF),
            pltpu.VMEM((C, ROWS), BF),
            pltpu.VMEM((ROWS, C), BF),
            pltpu.VMEM((C, ROWS), BF),
            pltpu.VMEM((2, 16, HALF), BF),
            pltpu.VMEM((2, HALF, ROWS), F32),
            pltpu.VMEM((2, 8, ROWS), F32),
            pltpu.VMEM((C, ROWS), F32),
            pltpu.VMEM((HEADS, 8, ROWS), F32),
            pltpu.VMEM((C, ROWS), BF),
            pltpu.VMEM((8, 128), F32),
            pltpu.VMEM((8, 128), F32),
            pltpu.SemaphoreType.DMA((10,)),
            pltpu.SemaphoreType.DMA((11,)),
            pltpu.SemaphoreType.DMA((11,)),
        ],
        compiler_params=pltpu.CompilerParams(
            collective_id=0, has_side_effects=True, vmem_limit_bytes=FRONT_VMEM
        ),
        name="front",
    )(
        points,
        voxel_index,
        counts,
        cpe_depth,
        cpe_weight,
        cpe_gain,
        norm1_gain,
        qkv_weight,
        proj_weight,
        norm2_gain,
    )
    return pl.pallas_call(
        back_kernel,
        out_shape=jax.ShapeDtypeStruct((1, ROWS, C), BF),
        in_specs=[hbm] * 4,
        out_specs=hbm,
        scratch_shapes=[
            pltpu.VMEM((ROWS, C), BF),
            pltpu.VMEM((8, C), F32),
            pltpu.VMEM((C, 4 * C), BF),
            pltpu.VMEM((4 * C, C), BF),
            pltpu.VMEM((ROWS, C), BF),
            pltpu.SemaphoreType.DMA((5,)),
        ],
        compiler_params=pltpu.CompilerParams(vmem_limit_bytes=BACK_VMEM),
        name="back",
    )(second, aside, mlp_in, mlp_out)


def solution(mesh):
    in_specs = (P("by", "bx", None), P("by", "bx"), P("by", "bx")) + (P(),) * 9
    return jax.shard_map(
        per_device,
        mesh=mesh,
        in_specs=in_specs,
        out_specs=P("by", "bx", None),
        check_vma=False,
    )
```

```python
import jax
import jax.numpy as jnp
from jax import lax
from jax.experimental import pallas as pl
from jax.experimental.pallas import tpu as pltpu
from jax.sharding import PartitionSpec as P

MESH = pl.DeviceIdType.MESH
BF = jnp.bfloat16
F32 = jnp.float32
C = 512
HEADS = 32
ROWS = 1024
HALF = 512
VX = 8
VY = 16
VZ = 16
VOX = 2048
PLANE = VY * VZ
NEG = -1e30
INNER = (VX - 2) * PLANE
EDGE = 2 * PLANE + (VX - 2) * 2 * VZ
CQ = 256
UNROLL = 8
FRONT_VMEM = 63 * 2**20
BACK_VMEM = 63 * 2**20


def dot(a, b):
    return jnp.dot(a, b, preferred_element_type=F32)


def dot_nt(a, b):
    return lax.dot_general(a, b, (((1,), (1,)), ((), ())), preferred_element_type=F32)


def dot_tn(a, b):
    return lax.dot_general(a, b, (((0,), (0,)), ((), ())), preferred_element_type=F32)


def layer_norm(values):
    center = values - jnp.mean(values, axis=-1, keepdims=True)
    spread = jnp.mean(center * center, axis=-1, keepdims=True)
    return center * lax.rsqrt(spread + 1e-05)


def front_kernel(
    points_hbm,
    voxels_hbm,
    counts_hbm,
    depth_hbm,
    cpe_w_hbm,
    cpe_gain_hbm,
    gain1_hbm,
    qkv_hbm,
    proj_hbm,
    gain2_hbm,
    second,
    aside,
    feats,
    voxels,
    counts,
    depth,
    cpe_gain,
    gain1,
    gain2,
    cpe_w,
    qkv_w,
    proj_w,
    wt,
    grid,
    face_out,
    face_in,
    taps,
    conv,
    edge_sum,
    edge,
    pos,
    first,
    normed,
    far,
    qt,
    keys,
    vt,
    far_keys,
    far_vt,
    ones,
    scores,
    tops,
    part_o,
    part_ml,
    att,
    count_out,
    count_in,
    load_sem,
    send_sem,
    recv_sem,
):
    bx, by = lax.axis_index("bx"), lax.axis_index("by")
    n_bx, n_by = lax.axis_size("bx"), lax.axis_size("by")
    low_x, high_x = lax.rem(bx + n_bx - 1, n_bx), lax.rem(bx + 1, n_bx)
    low_y, high_y = lax.rem(by + n_by - 1, n_by), lax.rem(by + 1, n_by)

    def at(x, y):
        return {"bx": x, "by": y}

    around = [
        (low_x, by),
        (high_x, by),
        (bx, low_y),
        (bx, high_y),
        (low_x, low_y),
        (low_x, high_y),
        (high_x, low_y),
        (high_x, high_y),
    ]
    barrier = pltpu.get_barrier_semaphore()
    for x, y in around:
        pl.semaphore_signal(barrier, inc=1, device_id=at(x, y), device_id_type=MESH)

    loads = [
        pltpu.make_async_copy(source, held, load_sem.at[i])
        for i, (source, held) in enumerate(
            (
                (voxels_hbm, voxels),
                (counts_hbm, counts),
                (points_hbm.at[0], feats),
                (depth_hbm, depth),
                (cpe_gain_hbm, cpe_gain),
                (gain1_hbm, gain1),
                (gain2_hbm, gain2),
                (cpe_w_hbm, cpe_w),
                (qkv_hbm, qkv_w),
                (proj_hbm, proj_w),
            )
        )
    ]
    for load in loads:
        load.start()

    def remote(i, source, target, where):
        return pltpu.make_async_remote_copy(
            src_ref=source,
            dst_ref=target,
            send_sem=send_sem.at[i],
            recv_sem=recv_sem.at[i],
            device_id=at(*where),
            device_id_type=MESH,
        )

    inner_y = pl.ds(1, VY)
    halo_x = [
        remote(0, grid.at[1, inner_y], grid.at[VX + 1, inner_y], (low_x, by)),
        remote(1, grid.at[VX, inner_y], grid.at[0, inner_y], (high_x, by)),
        remote(2, grid.at[1, 1], grid.at[VX + 1, VY + 1], (low_x, low_y)),
        remote(3, grid.at[1, VY], grid.at[VX + 1, 0], (low_x, high_y)),
        remote(4, grid.at[VX, 1], grid.at[0, VY + 1], (high_x, low_y)),
        remote(5, grid.at[VX, VY], grid.at[0, 0], (high_x, high_y)),
        remote(6, count_out, count_in, (high_x, by)),
    ]
    halo_y = [
        remote(7, face_out.at[0], face_in.at[1], (bx, low_y)),
        remote(8, face_out.at[1], face_in.at[0], (bx, high_y)),
    ]
    low_half, high_half = pl.ds(0, HALF), pl.ds(HALF, HALF)
    to_low = remote(9, normed.at[low_half], far.at[high_half], (low_x, by))
    to_high = remote(10, normed.at[high_half], far.at[low_half], (high_x, by))

    loads[0].wait()
    loads[1].wait()
    count = counts[...].astype(F32)
    count_out[...] = jnp.broadcast_to(count, (8, 128))
    slot = lax.broadcasted_iota(jnp.int32, (1, ROWS), 1)
    where_to = jnp.where(slot.astype(F32) < count, voxels[...], VOX)

    loads[2].wait()

    def scatter(first, second):
        row = lax.broadcasted_iota(jnp.int32, (2 * PLANE, ROWS), 0)
        row = row + jnp.where(row < PLANE, first * PLANE, (second - 1) * PLANE)
        hot = jnp.where(row == where_to, 1.0, 0.0).astype(BF)
        block = dot(hot, feats[...]).astype(BF).reshape(2, VY, VZ, C)
        for i, plane in enumerate((first, second)):
            grid[plane + 1, 1 : VY + 1] = block[i]
            face_out[0, plane] = block[i, 0]
            face_out[1, plane] = block[i, VY - 1]

    scatter(0, VX - 1)
    pl.semaphore_wait(barrier, 8)
    for copy in halo_x:
        copy.start()

    def scatter_step(i, carry):
        scatter(2 * i + 1, 2 * i + 2)
        return carry

    lax.fori_loop(0, VX // 2 - 1, scatter_step, 0)
    for copy in halo_y:
        copy.start()

    loads[3].wait()
    taps[...] = depth[...].astype(F32)

    z = lax.broadcasted_iota(jnp.int32, (VZ, 128), 0)

    def conv_rows(x, end, lanes, y_first, y_count, own):
        parts = [[None] * 3 for _ in range(y_count)]
        for off_x in range(3):
            x_out = off_x - 1 == end and end != 0
            for row in range(y_count + 2):
                y = y_first + row - 1
                y_out = y < 0 or y >= VY
                if own == (x_out or y_out):
                    continue
                if y_out and not x_out:
                    block = face_in[0 if y < 0 else 1, x + off_x - 1, :, lanes].astype(F32)
                else:
                    block = grid[x + off_x, y + 1, :, lanes].astype(F32)
                for i in range(y_count):
                    off_y = row - i
                    if 0 <= off_y <= 2:
                        for off_z in range(3):
                            term = block * taps[pl.ds(9 * off_x + 3 * off_y + off_z, 1), lanes]
                            held = parts[i][off_z]
                            parts[i][off_z] = term if held is None else held + term
        sums = []
        for before, same, after in parts:
            before = jnp.where(z == 0, 0.0, pltpu.roll(before, 1, 0))
            after = jnp.where(z == VZ - 1, 0.0, pltpu.roll(after, VZ - 1, 0))
            sums.append(before + same + after)
        return sums

    def edge_rows(x, end, y):
        if end:
            return pl.ds((0 if end < 0 else PLANE) + y * VZ, VZ)
        start = 2 * PLANE + (x - 1) * 2 * VZ + (0 if y == 0 else VZ)
        return pl.ds(pl.multiple_of(start, VZ), VZ)

    def lane_tile(i):
        return pl.ds(pl.multiple_of(i * 128, 128), 128)

    def inner_step(i, carry):
        lanes = lane_tile(lax.rem(i, 4))
        x = lax.div(i, 4) + 1
        for first_y in range(0, VY, 2):
            for y, total in enumerate(conv_rows(x, 0, lanes, first_y, 2, True), first_y):
                if y in (0, VY - 1):
                    edge_sum[edge_rows(x, 0, y), lanes] = total
                else:
                    start = pl.multiple_of((x - 1) * PLANE + y * VZ, VZ)
                    conv[pl.ds(start, VZ), lanes] = total.astype(BF)
        return carry

    lax.fori_loop(0, 4 * (VX - 2), inner_step, 0)

    def end_step(i, carry):
        lanes = lane_tile(i)
        for x, end in ((0, -1), (VX - 1, 1)):
            for first_y in range(0, VY, 2):
                for y, total in enumerate(conv_rows(x, end, lanes, first_y, 2, True), first_y):
                    edge_sum[edge_rows(x, end, y), lanes] = total
        return carry

    lax.fori_loop(0, 4, end_step, 0)

    for x in range(VX - 2):
        for y in (0, VY - 1):
            conv[x * PLANE + y * VZ : x * PLANE + (y + 1) * VZ] = jnp.zeros((VZ, C), BF)

    def one_hot(index, half, first, size):
        column = jnp.concatenate(
            [
                jnp.broadcast_to(index[:, half * HALF + i * 128 : half * HALF + (i + 1) * 128], (128, 128)).T
                for i in range(HALF // 128)
            ],
            axis=0,
        )
        pieces = [
            jnp.where(
                column == (lax.broadcasted_iota(jnp.int32, (1, 128), 1) + (first + i * 128)).astype(F32),
                1.0,
                0.0,
            ).astype(BF)
            for i in range(size // 128)
        ]
        return jnp.concatenate(pieces, axis=1)

    voxel = voxels[...]
    inner_index = (voxel - PLANE).astype(F32)
    for half in range(2):
        total = None
        for part in range(INNER // HALF):
            hot = one_hot(inner_index, half, part * HALF, HALF)
            term = dot(hot, conv[part * HALF : (part + 1) * HALF])
            total = term if total is None else total + term
        pos[half * HALF : (half + 1) * HALF] = total.astype(BF)

    for load in loads[4:]:
        load.wait()
    wt[0:C] = qkv_w[:, 0:C].T
    wt[C : 2 * C] = qkv_w[:, 2 * C : 3 * C].T

    for copy in halo_x + halo_y:
        copy.wait()
    zero_x = jnp.zeros((VY + 2, VZ, C), BF)
    zero_y = jnp.zeros((VX, VZ, C), BF)
    zero_row = jnp.zeros((VZ, C), BF)

    @pl.when(bx == 0)
    def _():
        grid[0] = zero_x

    @pl.when(bx == n_bx - 1)
    def _():
        grid[VX + 1] = zero_x

    @pl.when(by == 0)
    def _():
        face_in[0] = zero_y
        grid[0, 0] = zero_row
        grid[VX + 1, 0] = zero_row

    @pl.when(by == n_by - 1)
    def _():
        face_in[1] = zero_y
        grid[0, VY + 1] = zero_row
        grid[VX + 1, VY + 1] = zero_row

    def outer_step(i, carry):
        lanes = lane_tile(i)
        for x, end in ((0, -1), (VX - 1, 1)):
            for first_y in range(0, VY, 2):
                for y, total in enumerate(conv_rows(x, end, lanes, first_y, 2, False), first_y):
                    rows = edge_rows(x, end, y)
                    edge[rows, lanes] = (edge_sum[rows, lanes] + total).astype(BF)
        return carry

    lax.fori_loop(0, 4, outer_step, 0)

    def side_step(i, carry):
        lanes = lane_tile(lax.rem(i, 4))
        x = lax.div(i, 4) + 1
        for y in (0, VY - 1):
            rows = edge_rows(x, 0, y)
            total = conv_rows(x, 0, lanes, y, 1, False)[0]
            edge[rows, lanes] = (edge_sum[rows, lanes] + total).astype(BF)
        return carry

    lax.fori_loop(0, 4 * (VX - 2), side_step, 0)

    at_x, at_y = lax.div(voxel, PLANE), lax.rem(lax.div(voxel, VZ), VY)
    at_z = lax.rem(voxel, VZ)
    side = 2 * PLANE + (at_x - 1) * 2 * VZ + at_z
    edge_index = jnp.where(at_y == 0, side, jnp.where(at_y == VY - 1, side + VZ, -1))
    edge_index = jnp.where(at_x == VX - 1, voxel - (VX - 2) * PLANE, edge_index)
    edge_index = jnp.where(at_x == 0, voxel, edge_index).astype(F32)

    def gather(half):
        rows = slice(half * HALF, (half + 1) * HALF)
        total = pos[rows].astype(F32)
        total = total + dot(one_hot(edge_index, half, 0, 512), edge[0:512])
        total = total + dot(one_hot(edge_index, half, 512, 256)[:, : EDGE - 512], edge[512:EDGE])
        branch = layer_norm(dot(total.astype(BF), cpe_w[...])) * cpe_gain[...].reshape(1, C).astype(F32)
        here = (feats[rows].astype(F32) + branch).astype(BF)
        first[rows] = here
        normed[rows] = (layer_norm(here.astype(F32)) * gain1[...].reshape(1, C).astype(F32)).astype(BF)

    gather(0)
    to_low.start()
    gather(1)
    to_high.start()

    qt[...] = (dot_nt(wt[0:C], normed[...]).astype(BF).astype(F32) * 0.25).astype(BF)
    keys[...] = dot(normed[...], qkv_w[:, C : 2 * C]).astype(BF)
    vt[...] = dot_nt(wt[C : 2 * C], normed[...]).astype(BF)

    aside[0:1, :] = gain2[...].reshape(1, C).astype(F32)
    aside[1:2, :] = jnp.broadcast_to(count, (1, C))

    row_id = (lax.broadcasted_iota(jnp.int32, (HALF, 1), 0) + HALF).astype(F32)
    col_id = (lax.broadcasted_iota(jnp.int32, (1, HALF), 1) + HALF).astype(F32)

    def drop_invalid(k_ref, v_ref, start, total, which):
        here = slice(start, start + HALF)
        held = k_ref[here].astype(F32)
        k_ref[here] = jnp.where(row_id < total, held, held[0:1]).astype(BF)
        v_ref[:, here] = jnp.where(col_id < total, v_ref[:, here].astype(F32), 0.0).astype(BF)
        ones[which] = jnp.broadcast_to(jnp.where(col_id < total, 1.0, 0.0), (16, HALF)).astype(BF)

    drop_invalid(keys, vt, HALF, count, 0)

    lane_head = lax.broadcasted_iota(jnp.int32, (1, 128), 1) // 16
    all_ones = jnp.ones((16, HALF), BF)

    def attention(k_ref, v_ref, partial, which, finish):
        def step(h, before, now):
            other = 1 - now
            lanes = pl.ds(pl.multiple_of(lax.div(h, 8) * 128, 128), 128)
            mine = lane_head == lax.rem(h, 8)
            if before is not None:
                head_rows = pl.ds(pl.multiple_of(before * 16, 16), 16)
            for b in range(2):
                rows = slice(b * HALF, (b + 1) * HALF)
                k_h = k_ref[rows, lanes]
                k_h = jnp.where(mine, k_h, jnp.zeros_like(k_h))
                if before is not None:
                    counted = ones[which] if b == partial else all_ones
                    w = jnp.concatenate([v_ref[head_rows, rows], counted], axis=0)
                for part in range(HALF // CQ):
                    cols = slice(b * HALF + part * CQ, b * HALF + (part + 1) * CQ)
                    q_g = qt[lanes, cols]
                    s = dot(k_h, q_g)
                    scores[now, :, cols] = s
                    tops[now, 0:1, cols] = jnp.max(s, axis=0, keepdims=True)
                    if before is not None:
                        top = tops[other, 0:1, cols]
                        p = jnp.exp(scores[other, :, cols] - top).astype(BF)
                        finish(before, head_rows, cols, top, dot(w, p))

        step(0, None, 0)

        def body(i, carry):
            for u in range(UNROLL):
                before = i * UNROLL + u
                step(jnp.minimum(before + 1, HEADS - 1), before, (u + 1) % 2)
            return carry

        lax.fori_loop(0, HEADS // UNROLL, body, 0)

    def keep(h, head_rows, cols, top, acc):
        part_o[head_rows, cols] = acc[0:16]
        part_ml[h, 0:1, cols] = top
        part_ml[h, 1:2, cols] = acc[16:17]

    attention(keys, vt, 1, 0, keep)

    to_low.wait()
    to_high.wait()
    far_keys[...] = dot(far[...], qkv_w[:, C : 2 * C]).astype(BF)
    far_vt[...] = dot_nt(wt[C : 2 * C], far[...]).astype(BF)
    drop_invalid(far_keys, far_vt, 0, count_in[0:1, 0:1], 1)

    def merge(h, head_rows, cols, top, acc):
        near_top = part_ml[h, 0:1, cols]
        both = jnp.maximum(near_top, top)
        near, here = jnp.exp(near_top - both), jnp.exp(top - both)
        total = part_ml[h, 1:2, cols] * near + acc[16:17] * here
        att[head_rows, cols] = ((part_o[head_rows, cols] * near + acc[0:16] * here) / total).astype(BF)

    attention(far_keys, far_vt, 0, 1, merge)

    second[...] = (first[...].astype(F32) + dot_tn(att[...], proj_w[...])).astype(BF)


def gelu(x):
    half = 0.5 * x
    return half + half * lax.erf(x * 0.7071067811865476)


def back_kernel(second_hbm, aside_hbm, mlp_in_hbm, mlp_out_hbm, out_hbm, second, aside, mlp_in, mlp_out, out, sem):
    loads = [
        pltpu.make_async_copy(source, held, sem.at[i])
        for i, (source, held) in enumerate(
            (
                (second_hbm, second),
                (aside_hbm, aside),
                (mlp_in_hbm, mlp_in),
                (mlp_out_hbm, mlp_out),
            )
        )
    ]
    for load in loads:
        load.start()
    loads[0].wait()
    loads[1].wait()
    total = second[...].astype(F32)
    normed = (layer_norm(total) * aside[0:1, :]).astype(BF)
    loads[2].wait()
    for part in range(4):
        cols = slice(part * 512, (part + 1) * 512)
        hidden = gelu(dot(normed, mlp_in[:, cols])).astype(BF)
        if part == 0:
            loads[3].wait()
        total = total + dot(hidden, mlp_out[cols, :])
    row_id = lax.broadcasted_iota(jnp.int32, (ROWS, C), 0).astype(F32)
    out[...] = jnp.where(row_id < aside[1:2, :], total, 0.0).astype(BF)
    store = pltpu.make_async_copy(out, out_hbm.at[0], sem.at[4])
    store.start()
    store.wait()


def per_device(
    points,
    voxel_index,
    counts,
    cpe_depth,
    cpe_weight,
    cpe_gain,
    norm1_gain,
    qkv_weight,
    proj_weight,
    norm2_gain,
    mlp_in,
    mlp_out,
):
    vmem = pl.BlockSpec(memory_space=pltpu.VMEM)
    hbm = pl.BlockSpec(memory_space=pl.ANY)
    second, aside = pl.pallas_call(
        front_kernel,
        out_shape=(
            jax.ShapeDtypeStruct((ROWS, C), BF),
            jax.ShapeDtypeStruct((8, C), F32),
        ),
        in_specs=[hbm] * 10,
        out_specs=(vmem, vmem),
        scratch_shapes=[
            pltpu.VMEM((ROWS, C), BF),
            pltpu.VMEM((1, ROWS), jnp.int32),
            pltpu.VMEM((1, 1), jnp.int32),
            pltpu.VMEM((27, C), BF),
            pltpu.VMEM((C,), BF),
            pltpu.VMEM((C,), BF),
            pltpu.VMEM((C,), BF),
            pltpu.VMEM((C, C), BF),
            pltpu.VMEM((C, 3 * C), BF),
            pltpu.VMEM((C, C), BF),
            pltpu.VMEM((2 * C, C), BF),
            pltpu.VMEM((VX + 2, VY + 2, VZ, C), BF),
            pltpu.VMEM((2, VX, VZ, C), BF),
            pltpu.VMEM((2, VX, VZ, C), BF),
            pltpu.VMEM((27, C), F32),
            pltpu.VMEM((INNER, C), BF),
            pltpu.VMEM((EDGE, C), F32),
            pltpu.VMEM((EDGE, C), BF),
            pltpu.VMEM((ROWS, C), BF),
            pltpu.VMEM((ROWS, C), BF),
            pltpu.VMEM((ROWS, C), BF),
            pltpu.VMEM((ROWS, C), BF),
            pltpu.VMEM((C, ROWS), BF),
            pltpu.VMEM((ROWS, C), BF),
            pltpu.VMEM((C, ROWS), BF),
            pltpu.VMEM((ROWS, C), BF),
            pltpu.VMEM((C, ROWS), BF),
            pltpu.VMEM((2, 16, HALF), BF),
            pltpu.VMEM((2, HALF, ROWS), F32),
            pltpu.VMEM((2, 8, ROWS), F32),
            pltpu.VMEM((C, ROWS), F32),
            pltpu.VMEM((HEADS, 8, ROWS), F32),
            pltpu.VMEM((C, ROWS), BF),
            pltpu.VMEM((8, 128), F32),
            pltpu.VMEM((8, 128), F32),
            pltpu.SemaphoreType.DMA((10,)),
            pltpu.SemaphoreType.DMA((11,)),
            pltpu.SemaphoreType.DMA((11,)),
        ],
        compiler_params=pltpu.CompilerParams(
            collective_id=0, has_side_effects=True, vmem_limit_bytes=FRONT_VMEM
        ),
        name="front",
    )(
        points,
        voxel_index,
        counts,
        cpe_depth,
        cpe_weight,
        cpe_gain,
        norm1_gain,
        qkv_weight,
        proj_weight,
        norm2_gain,
    )
    return pl.pallas_call(
        back_kernel,
        out_shape=jax.ShapeDtypeStruct((1, ROWS, C), BF),
        in_specs=[hbm] * 4,
        out_specs=hbm,
        scratch_shapes=[
            pltpu.VMEM((ROWS, C), BF),
            pltpu.VMEM((8, C), F32),
            pltpu.VMEM((C, 4 * C), BF),
            pltpu.VMEM((4 * C, C), BF),
            pltpu.VMEM((ROWS, C), BF),
            pltpu.SemaphoreType.DMA((5,)),
        ],
        compiler_params=pltpu.CompilerParams(vmem_limit_bytes=BACK_VMEM),
        name="back",
    )(second, aside, mlp_in, mlp_out)


def solution(mesh):
    in_specs = (P("by", "bx", None), P("by", "bx"), P("by", "bx")) + (P(),) * 9
    return jax.shard_map(
        per_device,
        mesh=mesh,
        in_specs=in_specs,
        out_specs=P("by", "bx", None),
        check_vma=False,
    )
```
